512 devices in a mesh: dom: 64 (over z, y_hi, core), feat: 8 (over x, y_lo).
Axes of the slice: x: 4, y: 4 (y_hi: 2, y_lo: 2; y = y_hi * 2 + y_lo), z: 16, core: 2. Of those that a mesh axis runs over, the one named last changes fastest.
Arguments:
- node_features: bfloat16 [65536, 128], P('dom'), may hold values from -6 to 6
- weight: bfloat16 [128, 256], P(None, 'feat'), may hold values from -0.5 to 0.5
- bias: float32 [256], P('feat'), may hold values from -3 to 3
- tile_values: bfloat16 [6144, 128, 128], P('dom')
- tile_src: int32 [6144], P('dom'), may hold values from 0 to 7
- tile_dst: int32 [6144], P('dom'), may hold values from 0 to 31, as said below
- tile_counts: int32 [64], P('dom'), may hold values from 4 to 96
- out_grad: bfloat16 [65536, 256], P('dom', 'feat'), may hold values from -6 to 6
Outputs:
- output: bfloat16 [65536, 256], P('dom', 'feat')
- weight_grad: float32 [128, 256], P(None, 'feat')
- bias_grad: float32 [256], P('feat')
- input_grad: bfloat16 [65536, 128], P('dom', 'feat')
The draws below stay inside these ranges and needn't reach their ends.
Inputs may be any that keep to these rules, and one draw needn't show every extreme that they name: The partition offset tile_dst[k] // 8 of slot k of a partition equals k mod 4.
All inputs are finite; a program needn't handle non-finite values.
Results may differ from the reference program's by a relative error of at most 0.0075.
Values may be sent and summed in bfloat16 or wider, within the bound.
A program may use at most 64 MiB of HBM per device.

```python
import math
import jax
import jax.numpy as jnp
from jax import lax

F_IN = 128
HID = 256
BLOCK = 128
REACH = 4
NODE_DEV = 1024
CAP = 96
NB = 8
NODES = 65536
TILES = 6144
N_DOM = 64


def draw_tile_values(key, part):
    key = jax.random.fold_in(key, 11)
    mask_key, value_key = jax.random.split(key)
    present = (jax.random.randint(mask_key, (TILES, BLOCK, BLOCK), 0, 4) == 0).astype(jnp.float32)
    factor = 2.0 / math.sqrt(BLOCK * max(CAP // (NODE_DEV // BLOCK), 1))
    entries = jax.random.uniform(value_key, (TILES, BLOCK, BLOCK), jnp.float32, 0.5, 1.5)
    return (present * entries * factor).astype(jnp.bfloat16)


def draw_tile_dst(key, part):
    key = jax.random.fold_in(key, 12)
    blocks_dev = NODE_DEV // BLOCK
    within = jax.random.randint(key, (TILES,), 0, blocks_dev)
    slot_number = jnp.arange(TILES, dtype=jnp.int32) % CAP
    return (slot_number % REACH * blocks_dev + within).astype(jnp.int32)


def draw_tile_counts(key, part):
    key = jax.random.fold_in(key, 13)
    base_key, full_key, pick_key = jax.random.split(key, 3)
    lowest = max(REACH, CAP // 5)
    highest = max(lowest + 1, CAP // 2) + 1
    counts = jax.random.randint(base_key, (N_DOM,), lowest, highest)
    full = jax.random.randint(full_key, (N_DOM,), 0, 8) == 0
    chosen = jax.random.randint(pick_key, (), 0, N_DOM)
    full = full | (jnp.arange(N_DOM, dtype=jnp.int32) == chosen)
    return jnp.where(full, CAP, counts).astype(jnp.int32)


def with_ends(array, own_key, low, high):
    longest = array.shape.index(max(array.shape))
    spots = []
    for shift in (0, 1):
        where = [jax.random.randint(jax.random.fold_in(own_key, axis), (), 0, length) for axis, length in enumerate(array.shape)]
        where[longest] = (where[longest] + shift) % array.shape[longest]
        spots.append(tuple(where))
    return array.at[spots[0]].set(low).at[spots[1]].set(high)


def block_levels(own_key, extent, cuts, low, top_value):
    def one(position, shards_of):
        steps = jax.random.uniform(jax.random.fold_in(jax.random.fold_in(own_key, 6), position), (shards_of,), jnp.float32, low / len(cuts), top_value / len(cuts))
        return jnp.repeat(jnp.exp(steps), extent[position] // shards_of).reshape((-1,) + (1,) * (len(extent) - position - 1))

    level = one(*cuts[0])
    for cut in cuts[1:]:
        level = level * one(*cut)
    return level


def centred(stream_key, shape, width, bound, cuts=(), kind=jnp.bfloat16):
    values = width * jax.random.normal(stream_key, shape, jnp.float32)
    if cuts:
        values = values * block_levels(stream_key, shape, cuts, -0.22, 0.18)
    return jnp.clip(values, -bound, bound).astype(kind)


def setup_inputs(seed: int = 0) -> dict:
    arg_keys = jax.random.split(jax.random.key(seed), 9)
    node_features = centred(arg_keys[0], (NODES, F_IN), 1.0, 6.0, ((0, 64),))
    weight = centred(arg_keys[1], (F_IN, HID), F_IN ** -0.5, 0.5, ((1, 8),))
    bias = centred(arg_keys[2], (HID,), 0.5, 3.0, ((0, 8),), jnp.float32)
    tile_values = draw_tile_values(jax.random.fold_in(arg_keys[8], 71), 0)
    tile_src = with_ends(jax.random.randint(arg_keys[4], (TILES,), 0, NB), jax.random.fold_in(arg_keys[4], 1), 0, NB - 1).astype(jnp.int32)
    tile_dst = draw_tile_dst(jax.random.fold_in(arg_keys[8], 71), 0)
    tile_counts = draw_tile_counts(jax.random.fold_in(arg_keys[8], 71), 0)
    out_grad = centred(arg_keys[7], (NODES, HID), 1.0, 6.0, ((0, 64), (1, 8)))
    return dict(node_features=node_features, weight=weight, bias=bias, tile_values=tile_values, tile_src=tile_src, tile_dst=tile_dst, tile_counts=tile_counts, out_grad=out_grad)


def reference(node_features, weight, bias, tile_values, tile_src, tile_dst, tile_counts, out_grad):
    blocks_dev = NODE_DEV // BLOCK
    all_blocks = blocks_dev * N_DOM
    projected = jnp.dot(node_features, weight, preferred_element_type=jnp.float32).astype(jnp.bfloat16)
    proj_blocks = projected.reshape(all_blocks, BLOCK, HID)
    values_dev = tile_values.reshape(N_DOM, CAP, BLOCK, BLOCK)
    src_dev = tile_src.reshape(N_DOM, CAP)
    dst_dev = tile_dst.reshape(N_DOM, CAP)
    owners = jnp.arange(N_DOM, dtype=jnp.int32)
    slots = jnp.arange(CAP, dtype=jnp.int32)

    def indices(owner, sources, targets, used):
        src_global = (owner * blocks_dev + sources).astype(jnp.int32)
        dst_global = (((owner + targets // blocks_dev) % N_DOM) * blocks_dev + targets % blocks_dev).astype(jnp.int32)
        live_slots = (slots < used).astype(jnp.float32)
        return src_global, dst_global, live_slots

    def forward_step(running, items):
        owner, tiles, sources, targets, used = items
        src_global, dst_global, live_slots = indices(owner, sources, targets, used)
        terms = jnp.einsum("kij,kjf->kif", tiles.astype(jnp.float32), proj_blocks[src_global].astype(jnp.float32))
        return running.at[dst_global].add(terms * live_slots[:, None, None]), None

    start = jnp.zeros((all_blocks, BLOCK, HID), jnp.float32)
    aggregated, _ = lax.scan(forward_step, start, (owners, values_dev, src_dev, dst_dev, tile_counts))
    pre = aggregated.reshape(NODE_DEV * N_DOM, HID) + bias[None, :]
    output = jax.nn.silu(pre).astype(jnp.bfloat16)
    sigmoid_pre = jax.nn.sigmoid(pre)
    grad_pre = (out_grad.astype(jnp.float32) * sigmoid_pre * (1.0 + pre * (1.0 - sigmoid_pre))).astype(jnp.bfloat16)
    grad_blocks = grad_pre.reshape(all_blocks, BLOCK, HID)

    def backward_step(running, items):
        owner, tiles, sources, targets, used = items
        src_global, dst_global, live_slots = indices(owner, sources, targets, used)
        terms = jnp.einsum("kji,kjf->kif", tiles.astype(jnp.float32), grad_blocks[dst_global].astype(jnp.float32))
        return running.at[src_global].add(terms * live_slots[:, None, None]), None

    upstream, _ = lax.scan(backward_step, start, (owners, values_dev, src_dev, dst_dev, tile_counts))
    upstream = upstream.reshape(NODE_DEV * N_DOM, HID).astype(jnp.bfloat16)
    weight_grad = jnp.dot(node_features.T, upstream, preferred_element_type=jnp.float32)
    bias_grad = jnp.sum(grad_pre.astype(jnp.float32), axis=0)
    input_grad = jnp.dot(upstream, weight.T, preferred_element_type=jnp.float32).astype(jnp.bfloat16)
    return output, weight_grad, bias_grad, input_grad
```

```python
import functools

import jax
import jax.numpy as jnp
from jax import lax
from jax.experimental import pallas as pl
from jax.experimental.pallas import tpu as pltpu
from jax.sharding import PartitionSpec as P

REACH = 4
NB = 8
BLOCK = 128
NFEAT = 8
FW = 16
PER_OFFSET = 24
HID_DEV = 32
GROUP = 4
MESH = pl.DeviceIdType.MESH
F32 = jnp.float32
BF16 = jnp.bfloat16
ORDER = (3, 2, 1, 0)


def kernel(
    n_dom,
    nf_hbm, wt, bias, tiles_hbm, src, dst, cnt, og_hbm,
    out, wg, bg, ig,
    nf, og, tiles, nft, table, psend, precv, agg, hsend, hrecv, hall0, hall1, hall2, hall3,
    rsend, rrecv, zbuf, wfin,
    load_sem, tile_sem, p_sem, a_sem, h_sem, b_sem, r_sem, z_sem, w_sem,
):
    n_z = n_dom // GROUP
    hall = (hall0, hall1, hall2, hall3)
    dom = lax.axis_index("dom")
    feat = lax.axis_index("feat")
    z = dom // GROUP
    lane = lax.rem(dom, GROUP)

    def dom_at(step):
        return lax.rem(dom + (step % n_dom), n_dom)

    def feat_at(step):
        return lax.rem(feat + step, NFEAT)

    def group_at(step):
        return lax.rem(lane + step, GROUP)

    def z_at(step):
        return lax.rem(z + step, n_z)

    barrier = pltpu.get_barrier_semaphore()

    def greet(device):
        pl.semaphore_signal(barrier, inc=1, device_id=device, device_id_type=MESH)

    loads = [
        pltpu.make_async_copy(nf_hbm, nf, load_sem.at[0]),
        pltpu.make_async_copy(og_hbm, og, load_sem.at[1]),
    ]
    tile_loads = {
        o: pltpu.make_async_copy(tiles_hbm.at[:, o], tiles.at[o], tile_sem.at[o])
        for o in range(REACH)
    }
    loads[0].start()
    for o in ORDER:
        tile_loads[o].start()
    loads[1].start()

    for step in range(1, REACH):
        greet((dom_at(step), feat))
        greet((dom_at(-step), feat))
    for step in range(1, NFEAT):
        greet((dom, feat_at(step)))
    for step in range(1, n_z):
        greet((z_at(step) * GROUP + lane, feat))
    greetings = 2 * (REACH - 1) + NFEAT - 1 + n_z - 1

    def send(src_ref, dst_ref, sems, s, r, device):
        copy = pltpu.make_async_remote_copy(
            src_ref=src_ref,
            dst_ref=dst_ref,
            send_sem=sems.at[0, s],
            recv_sem=sems.at[1, r],
            device_id=device,
            device_id_type=MESH,
        )
        copy.start()
        return copy

    def arrival(ref, sems, r):
        pltpu.make_async_copy(ref, ref, sems.at[1, r]).wait()

    one = jnp.ones((FW, BLOCK), BF16)
    zero = jnp.zeros((FW, BLOCK), BF16)
    for g in range(NB + 1):
        for row in range(NB):
            table[g, row * FW : (row + 1) * FW, :] = one if row == g else zero

    loads[0].wait()
    rows = lax.broadcasted_iota(jnp.int32, (FW, BLOCK), 0)
    columns = lax.broadcasted_iota(jnp.int32, (FW, BLOCK), 1)
    pick = jnp.where(columns == rows + feat * FW, 1.0, 0.0).astype(BF16)
    picked = lax.dot_general(
        pick, nf[...], (((1,), (1,)), ((), ())), preferred_element_type=F32
    ).astype(BF16)
    for b in range(NB):
        nft[b] = picked[:, b * BLOCK : (b + 1) * BLOCK]

    used = cnt[0]

    def placed(block, position, k):
        position = jnp.where(k < used, position, NB)
        return jnp.concatenate([block] * NB, axis=0) * table[position]

    def forward(o):
        left = []
        right = []
        for j in range(PER_OFFSET):
            k = j * REACH + o
            left.append(placed(nft[src[k]], dst[k] & (NB - 1), k))
            right.append(tiles[o, j])
        return lax.dot_general(
            jnp.concatenate(left, axis=1),
            jnp.concatenate(right, axis=1),
            (((1,), (1,)), ((), ())),
            preferred_element_type=F32,
        )

    sends = []
    own = None
    for o in ORDER:
        tile_loads[o].wait()
        part = forward(o)
        if o == 0:
            own = part
        else:
            psend[o - 1] = part.astype(BF16)
            if o == ORDER[0]:
                pl.semaphore_wait(barrier, greetings)
            sends.append(
                send(psend.at[o - 1], precv.at[o - 1], p_sem, o - 1, o - 1, (dom_at(o), feat))
            )
    for o in ORDER:
        if o:
            arrival(precv.at[o - 1], p_sem, o - 1)
            own = own + precv[o - 1].astype(F32)
    agg[feat] = own.astype(BF16)
    for step in range(1, NFEAT):
        sends.append(
            send(agg.at[feat], agg.at[feat], a_sem, step, feat, (dom, feat_at(step)))
        )
    loads[1].wait()
    bias_square = jnp.broadcast_to(bias[...], (HID_DEV, HID_DEV))
    on_diagonal = lax.broadcasted_iota(jnp.int32, (HID_DEV, HID_DEV), 0) == (
        lax.broadcasted_iota(jnp.int32, (HID_DEV, HID_DEV), 1)
    )
    bias_column = jnp.sum(jnp.where(on_diagonal, bias_square, 0.0), axis=1, keepdims=True)
    for step in range(1, NFEAT):
        arrival(agg.at[feat_at(step)], a_sem, feat_at(step))
    aggregated = jnp.concatenate(
        [
            jnp.concatenate([agg[i, g * FW : (g + 1) * FW, :] for i in range(NFEAT)], axis=0)
            for g in range(NB)
        ],
        axis=1,
    )
    pre = (
        jnp.dot(wt[...], aggregated, preferred_element_type=F32) + bias_column
    )
    sigmoid_pre = jax.nn.sigmoid(pre)
    grad_pre = (
        og[...].astype(F32) * sigmoid_pre * (1.0 + pre * (1.0 - sigmoid_pre))
    ).astype(BF16)
    back = lax.dot_general(
        wt[...], grad_pre, (((0,), (0,)), ((), ())), preferred_element_type=F32
    ).astype(BF16)
    for i in range(NFEAT):
        for g in range(NB):
            hsend[i, g * FW : (g + 1) * FW, :] = back[
                i * FW : (i + 1) * FW, g * BLOCK : (g + 1) * BLOCK
            ]
    for step in range(1, NFEAT):
        sends.append(
            send(
                hsend.at[feat_at(step)], hrecv.at[feat], h_sem, step, feat, (dom, feat_at(step))
            )
        )
    hrecv[feat] = hsend[feat]
    out[...] = (pre * sigmoid_pre).astype(BF16)

    weight_part = lax.dot_general(
        grad_pre, aggregated, (((1,), (1,)), ((), ())), preferred_element_type=F32
    )
    bias_part = lax.dot_general(
        jnp.ones((8, NB * BLOCK), BF16),
        jnp.concatenate([grad_pre] * 4, axis=0),
        (((1,), (1,)), ((), ())),
        preferred_element_type=F32,
    )
    for c in range(GROUP):
        rsend[c, 0:8, :] = weight_part[c * 8 : (c + 1) * 8, :]
        rsend[c, 8:16, :] = bias_part
    for step in range(1, GROUP):
        sends.append(
            send(
                rsend.at[group_at(step)], rrecv.at[lane], r_sem, step, lane,
                (z * GROUP + group_at(step), feat),
            )
        )
    rrecv[lane] = rsend[lane]

    for step in range(1, NFEAT):
        arrival(hrecv.at[feat_at(step)], h_sem, feat_at(step))
    mixed = hrecv[0].astype(F32)
    for i in range(1, NFEAT):
        mixed = mixed + hrecv[i].astype(F32)
    mixed = mixed.astype(BF16)
    for g in range(NB):
        hall0[g] = mixed[g * FW : (g + 1) * FW, :]
    for o in ORDER[:-1]:
        sends.append(
            send(hall0, hall[o], b_sem, o, o, (dom_at(-o), feat))
        )

    for step in range(1, GROUP):
        arrival(rrecv.at[group_at(step)], r_sem, group_at(step))
    zbuf[z] = jnp.sum(rrecv[...], axis=0)
    for step in range(1, n_z):
        sends.append(
            send(zbuf.at[z], zbuf.at[z], z_sem, step, z, (z_at(step) * GROUP + lane, feat))
        )

    def backward(o):
        left = []
        for j in range(PER_OFFSET):
            k = j * REACH + o
            left.append(placed(hall[o][dst[k] & (NB - 1)], src[k], k))
        return jnp.dot(
            jnp.concatenate(left, axis=1),
            tiles[o].reshape(PER_OFFSET * BLOCK, BLOCK),
            preferred_element_type=F32,
        )

    total = backward(0)
    for o in (1, 2):
        arrival(hall[o], b_sem, o)
        total = total + backward(o)

    for step in range(1, n_z):
        arrival(zbuf.at[z_at(step)], z_sem, z_at(step))
    wfin[lane] = jnp.sum(zbuf[...], axis=0)
    for step in range(1, GROUP):
        sends.append(
            send(
                wfin.at[lane], wfin.at[lane], w_sem, step, lane,
                (z * GROUP + group_at(step), feat),
            )
        )
    arrival(hall3, b_sem, 3)
    total = (total + backward(3)).astype(BF16)
    for g in range(NB):
        ig[:, g * BLOCK : (g + 1) * BLOCK] = total[g * FW : (g + 1) * FW, :]
    for step in range(1, GROUP):
        arrival(wfin.at[group_at(step)], w_sem, group_at(step))
    for c in range(GROUP):
        wg[c * 8 : (c + 1) * 8, :] = wfin[c, 0:8, :]
    bg[...] = wfin[0, 8:9, 0:HID_DEV]
    for copy in sends:
        copy.wait_send()


def shards(node_features, weight, bias, tile_values, tile_src, tile_dst, tile_counts, out_grad):
    n_dom = lax.axis_size("dom")
    n_z = n_dom // GROUP
    nodes = NB * BLOCK
    vmem = pl.BlockSpec(memory_space=pltpu.VMEM)
    smem = pl.BlockSpec(memory_space=pltpu.SMEM)
    hbm = pl.BlockSpec(memory_space=pltpu.HBM)
    dma = pltpu.SemaphoreType.DMA
    out, wg, bg, ig = pl.pallas_call(
        functools.partial(kernel, n_dom),
        out_shape=(
            jax.ShapeDtypeStruct((HID_DEV, nodes), BF16),
            jax.ShapeDtypeStruct((HID_DEV, BLOCK), F32),
            jax.ShapeDtypeStruct((1, HID_DEV), F32),
            jax.ShapeDtypeStruct((FW, nodes), BF16),
        ),
        in_specs=[hbm, vmem, vmem, hbm, smem, smem, smem, hbm],
        out_specs=(vmem, vmem, vmem, vmem),
        scratch_shapes=[
            pltpu.VMEM((nodes, BLOCK), BF16),
            pltpu.VMEM((HID_DEV, nodes), BF16),
            pltpu.VMEM((REACH, PER_OFFSET, BLOCK, BLOCK), BF16),
            pltpu.VMEM((NB, FW, BLOCK), BF16),
            pltpu.VMEM((NB + 1, BLOCK, BLOCK), BF16),
            pltpu.VMEM((REACH - 1, BLOCK, BLOCK), BF16),
            pltpu.VMEM((REACH - 1, BLOCK, BLOCK), BF16),
            pltpu.VMEM((NFEAT, BLOCK, BLOCK), BF16),
            pltpu.VMEM((NFEAT, BLOCK, BLOCK), BF16),
            pltpu.VMEM((NFEAT, BLOCK, BLOCK), BF16),
            pltpu.VMEM((NB, FW, BLOCK), BF16),
            pltpu.VMEM((NB, FW, BLOCK), BF16),
            pltpu.VMEM((NB, FW, BLOCK), BF16),
            pltpu.VMEM((NB, FW, BLOCK), BF16),
            pltpu.VMEM((GROUP, 16, BLOCK), F32),
            pltpu.VMEM((GROUP, 16, BLOCK), F32),
            pltpu.VMEM((n_z, 16, BLOCK), F32),
            pltpu.VMEM((GROUP, 16, BLOCK), F32),
            dma((2,)),
            dma((REACH,)),
            dma((2, REACH - 1)),
            dma((2, NFEAT)),
            dma((2, NFEAT)),
            dma((2, REACH)),
            dma((2, GROUP)),
            dma((2, n_z)),
            dma((2, GROUP)),
        ],
        compiler_params=pltpu.CompilerParams(
            collective_id=0, has_side_effects=True
        ),
        name="graph_layer",
    )(
        node_features,
        weight.T,
        bias.reshape(1, HID_DEV),
        tile_values.reshape(PER_OFFSET, REACH, BLOCK, BLOCK),
        tile_src,
        tile_dst,
        tile_counts,
        out_grad.T,
    )
    return out.T, wg.T, bg.reshape(HID_DEV), ig.T


def solution(mesh):
    return jax.shard_map(
        shards,
        mesh=mesh,
        in_specs=(
            P("dom", None),
            P(None, "feat"),
            P("feat"),
            P("dom", None, None),
            P("dom"),
            P("dom"),
            P("dom"),
            P("dom", "feat"),
        ),
        out_specs=(P("dom", "feat"), P(None, "feat"), P("feat"), P("dom", "feat")),
        check_vma=False,
    )
```

```python
import functools

import jax
import jax.numpy as jnp
from jax import lax
from jax.experimental import pallas as pl
from jax.experimental.pallas import tpu as pltpu
from jax.sharding import PartitionSpec as P

REACH = 4
NB = 8
BLOCK = 128
NFEAT = 8
FW = 16
PER_OFFSET = 24
HID_DEV = 32
GROUP = 4
MESH = pl.DeviceIdType.MESH
F32 = jnp.float32
BF16 = jnp.bfloat16
ORDER = (3, 2, 1, 0)


def kernel(
    n_dom,
    nf_hbm, wt_hbm, bias_hbm, tiles_hbm, src_hbm, dst_hbm, cnt, og_hbm,
    out, wg, bg, ig,
    nf, og, wt, bias, src, dst, tiles, nft, table, psend, precv, agg, hsend, hrecv,
    hall0, hall1, hall2, hall3,
    rsend, rrecv, rbias, ysend, yrecv, ybias, zbuf, zbias, wfin,
    load_sem, tile_sem, p_sem, a_sem, h_sem, b_sem, r_sem, y_sem, z_sem, zb_sem, w_sem,
    relay_sem,
):
    n_z = n_dom // GROUP
    hall = (hall0, hall1, hall2, hall3)
    dom = lax.axis_index("dom")
    feat = lax.axis_index("feat")
    z = dom // GROUP
    lane = lax.rem(dom, GROUP)
    core = lax.rem(dom, 2)
    partner = (dom + 1 - 2 * core, feat)
    across = (z * GROUP + lax.rem(lane + 2, GROUP), feat)

    def dom_at(step):
        return lax.rem(dom + (step % n_dom), n_dom)

    def feat_at(step):
        return lax.rem(feat + step, NFEAT)

    def z_at(step):
        return lax.rem(z + step, n_z)

    def z_peer(step):
        return (z_at(step) * GROUP + lane, feat)

    def around(*distances):
        return sorted({d % n_z for r in distances for d in (r, -r)} - {0})

    barrier = pltpu.get_barrier_semaphore()

    def signal(sem, device):
        pl.semaphore_signal(sem, inc=1, device_id=device, device_id_type=MESH)

    near = [(dom_at(step), feat) for step in range(1, REACH)]
    near += [(dom_at(-step), feat) for step in range(1, REACH)]
    near += [(dom, feat_at(step)) for step in range(1, NFEAT)]
    near += [z_peer(step) for step in around(1, 2)]
    for device in near:
        signal(barrier, device)

    pairs = [
        (src_hbm, src), (dst_hbm, dst), (nf_hbm, nf),
        (wt_hbm, wt), (bias_hbm, bias), (og_hbm, og),
    ]
    loads = [pltpu.make_async_copy(a, b, load_sem.at[i]) for i, (a, b) in enumerate(pairs)]
    tile_loads = [
        pltpu.make_async_copy(tiles_hbm.at[:, o], tiles.at[o], tile_sem.at[o])
        for o in range(REACH)
    ]
    for load in loads[:3]:
        load.start()
    for o in ORDER:
        tile_loads[o].start()
    for load in loads[3:]:
        load.start()

    sends = []

    def send(src_ref, dst_ref, sems, s, r, device):
        copy = pltpu.make_async_remote_copy(
            src_ref=src_ref,
            dst_ref=dst_ref,
            send_sem=sems.at[0, s],
            recv_sem=sems.at[1, r],
            device_id=device,
            device_id_type=MESH,
        )
        copy.start()
        sends.append(copy)

    def arrival(ref, sems, r):
        pltpu.make_async_copy(ref, ref, sems.at[1, r]).wait()

    one = jnp.ones((FW, BLOCK), BF16)
    zero = jnp.zeros((FW, BLOCK), BF16)
    for g in range(NB + 1):
        for row in range(NB):
            table[g, row * FW : (row + 1) * FW, :] = one if row == g else zero

    rows = lax.broadcasted_iota(jnp.int32, (FW, BLOCK), 0)
    columns = lax.broadcasted_iota(jnp.int32, (FW, BLOCK), 1)
    pick = jnp.where(columns == rows + feat * FW, 1.0, 0.0).astype(BF16)
    for load in loads[:3]:
        load.wait()
    picked = lax.dot_general(
        pick, nf[...], (((1,), (1,)), ((), ())), preferred_element_type=F32
    ).astype(BF16)
    for b in range(NB):
        nft[b] = picked[:, b * BLOCK : (b + 1) * BLOCK]

    used = cnt[0]

    def placed(block, position, k):
        position = jnp.where(k < used, position, NB)
        return jnp.concatenate([block] * NB, axis=0) * table[position]

    def forward(o):
        left = []
        right = []
        for j in range(PER_OFFSET):
            k = j * REACH + o
            left.append(placed(nft[src[k]], dst[k] & (NB - 1), k))
            right.append(tiles[o, j])
        return lax.dot_general(
            jnp.concatenate(left, axis=1),
            jnp.concatenate(right, axis=1),
            (((1,), (1,)), ((), ())),
            preferred_element_type=F32,
        )

    for o in ORDER[:-1]:
        tile_loads[o].wait()
        psend[o - 1] = forward(o).astype(BF16)
    tile_loads[0].wait()
    own = forward(0)
    for load in loads[3:]:
        load.wait()
    pl.semaphore_wait(barrier, len(near))
    for o in ORDER[:-1]:
        send(psend.at[o - 1], precv.at[o - 1], p_sem, o - 1, o - 1, (dom_at(o), feat))
    for step in around(2):
        signal(relay_sem.at[0], z_peer(step))
    bias_square = jnp.broadcast_to(bias[...], (HID_DEV, HID_DEV))
    on_diagonal = lax.broadcasted_iota(jnp.int32, (HID_DEV, HID_DEV), 0) == (
        lax.broadcasted_iota(jnp.int32, (HID_DEV, HID_DEV), 1)
    )
    bias_column = jnp.sum(jnp.where(on_diagonal, bias_square, 0.0), axis=1, keepdims=True)
    for o in ORDER[:-1]:
        arrival(precv.at[o - 1], p_sem, o - 1)
        own = own + precv[o - 1].astype(F32)
    agg[feat] = own.astype(BF16)
    for step in range(1, NFEAT):
        send(agg.at[feat], agg.at[feat], a_sem, step, feat, (dom, feat_at(step)))
    if around(2):
        pl.semaphore_wait(relay_sem.at[0], len(around(2)))
    for step in around(4):
        signal(relay_sem.at[1], z_peer(step))
    for step in range(1, NFEAT):
        arrival(agg.at[feat_at(step)], a_sem, feat_at(step))
    aggregated = jnp.concatenate(
        [
            jnp.concatenate([agg[i, g * FW : (g + 1) * FW, :] for i in range(NFEAT)], axis=0)
            for g in range(NB)
        ],
        axis=1,
    )
    pre = jnp.dot(wt[...], aggregated, preferred_element_type=F32) + bias_column
    sigmoid_pre = jax.nn.sigmoid(pre)
    grad_pre = (
        og[...].astype(F32) * sigmoid_pre * (1.0 + pre * (1.0 - sigmoid_pre))
    ).astype(BF16)

    weight_part = lax.dot_general(
        grad_pre, aggregated, (((1,), (1,)), ((), ())), preferred_element_type=F32
    )
    bias_part = lax.dot_general(
        jnp.ones((8, NB * BLOCK), BF16),
        jnp.concatenate([grad_pre] * 4, axis=0),
        (((1,), (1,)), ((), ())),
        preferred_element_type=F32,
    )
    rsend[0] = weight_part[0:16, :]
    rsend[1] = weight_part[16:32, :]
    rbias[0] = bias_part[0:1, :]
    send(rsend.at[1 - core], rrecv, r_sem, 0, 0, partner)
    send(rbias.at[0], rbias.at[1], r_sem, 1, 1, partner)

    back = lax.dot_general(
        wt[...], grad_pre, (((0,), (0,)), ((), ())), preferred_element_type=F32
    ).astype(BF16)
    for i in range(NFEAT):
        for g in range(NB):
            hsend[i, g * FW : (g + 1) * FW, :] = back[
                i * FW : (i + 1) * FW, g * BLOCK : (g + 1) * BLOCK
            ]
    for step in range(1, NFEAT):
        send(hsend.at[feat_at(step)], hrecv.at[feat], h_sem, step, feat, (dom, feat_at(step)))
    hrecv[feat] = hsend[feat]

    arrival(rrecv, r_sem, 0)
    arrival(rbias.at[1], r_sem, 1)
    ysend[...] = rsend[core] + rrecv[...]
    ybias[0] = rbias[0] + rbias[1]
    send(ysend, yrecv, y_sem, 0, 0, across)
    send(ybias.at[0], ybias.at[1], y_sem, 1, 1, across)
    out[...] = (pre * sigmoid_pre).astype(BF16)
    if around(4):
        pl.semaphore_wait(relay_sem.at[1], len(around(4)))
    arrival(yrecv, y_sem, 0)
    arrival(ybias.at[1], y_sem, 1)
    zbuf[z] = (ysend[...] + yrecv[...]).astype(BF16)
    zbias[z] = ybias[0] + ybias[1]
    for step in range(1, n_z):
        send(zbuf.at[z], zbuf.at[z], z_sem, step, z, z_peer(step))
        send(zbias.at[z], zbias.at[z], zb_sem, step, z, z_peer(step))

    for step in range(1, NFEAT):
        arrival(hrecv.at[feat_at(step)], h_sem, feat_at(step))
    mixed = hrecv[0].astype(F32)
    for i in range(1, NFEAT):
        mixed = mixed + hrecv[i].astype(F32)
    mixed = mixed.astype(BF16)
    for g in range(NB):
        hall0[g] = mixed[g * FW : (g + 1) * FW, :]
    for o in ORDER[:-1]:
        send(hall0, hall[o], b_sem, o, o, (dom_at(-o), feat))

    def backward(o):
        left = []
        for j in range(PER_OFFSET):
            k = j * REACH + o
            left.append(placed(hall[o][dst[k] & (NB - 1)], src[k], k))
        return jnp.dot(
            jnp.concatenate(left, axis=1),
            tiles[o].reshape(PER_OFFSET * BLOCK, BLOCK),
            preferred_element_type=F32,
        )

    total = backward(0)
    for o in (1, 2, 3):
        arrival(hall[o], b_sem, o)
        total = total + backward(o)
    total = total.astype(BF16)
    for g in range(NB):
        ig[:, g * BLOCK : (g + 1) * BLOCK] = total[g * FW : (g + 1) * FW, :]

    for step in range(1, n_z):
        arrival(zbuf.at[z_at(step)], z_sem, z_at(step))
    wfin[core] = jnp.sum(zbuf[...].astype(F32), axis=0)
    send(wfin.at[core], wfin.at[core], w_sem, 0, core, partner)
    for step in range(1, n_z):
        arrival(zbias.at[z_at(step)], zb_sem, z_at(step))
    bg[...] = jnp.sum(zbias[...], axis=0)[:, 0:HID_DEV]
    arrival(wfin.at[1 - core], w_sem, 1 - core)
    wg[0:16, :] = wfin[0]
    wg[16:32, :] = wfin[1]
    for copy in sends:
        copy.wait_send()


def finish(*refs):
    values, outs, sem = refs[:4], refs[4:8], refs[8]
    copies = [pltpu.make_async_copy(a, b, sem.at[i]) for i, (a, b) in enumerate(zip(values, outs))]
    for copy in copies:
        copy.start()
    for copy in copies:
        copy.wait()


def shards(node_features, weight, bias, tile_values, tile_src, tile_dst, tile_counts, out_grad):
    n_dom = lax.axis_size("dom")
    n_z = n_dom // GROUP
    nodes = NB * BLOCK
    vmem = pl.BlockSpec(memory_space=pltpu.VMEM)
    hbm = pl.BlockSpec(memory_space=pltpu.HBM)
    anywhere = pl.BlockSpec(memory_space=pl.ANY)
    dma = pltpu.SemaphoreType.DMA
    block = pltpu.VMEM((NB, FW, BLOCK), BF16)
    square = pltpu.VMEM((NFEAT, BLOCK, BLOCK), BF16)
    limit = 24 * 1024 * 1024
    shapes = (
        jax.ShapeDtypeStruct((HID_DEV, nodes), BF16),
        jax.ShapeDtypeStruct((HID_DEV, BLOCK), F32),
        jax.ShapeDtypeStruct((1, HID_DEV), F32),
        jax.ShapeDtypeStruct((FW, nodes), BF16),
    )
    results = pl.pallas_call(
        functools.partial(kernel, n_dom),
        out_shape=shapes,
        in_specs=[hbm] * 6 + [pl.BlockSpec(memory_space=pltpu.SMEM), hbm],
        out_specs=(vmem,) * 4,
        scratch_shapes=[
            pltpu.VMEM((nodes, BLOCK), BF16),
            pltpu.VMEM((HID_DEV, nodes), BF16),
            pltpu.VMEM((HID_DEV, BLOCK), BF16),
            pltpu.VMEM((1, HID_DEV), F32),
            pltpu.SMEM((PER_OFFSET * REACH,), jnp.int32),
            pltpu.SMEM((PER_OFFSET * REACH,), jnp.int32),
            pltpu.VMEM((REACH, PER_OFFSET, BLOCK, BLOCK), BF16),
            block,
            pltpu.VMEM((NB + 1, BLOCK, BLOCK), BF16),
            pltpu.VMEM((REACH - 1, BLOCK, BLOCK), BF16),
            pltpu.VMEM((REACH - 1, BLOCK, BLOCK), BF16),
            square,
            square,
            square,
            block,
            block,
            block,
            block,
            pltpu.VMEM((2, 16, BLOCK), F32),
            pltpu.VMEM((16, BLOCK), F32),
            pltpu.VMEM((2, 1, BLOCK), F32),
            pltpu.VMEM((16, BLOCK), F32),
            pltpu.VMEM((16, BLOCK), F32),
            pltpu.VMEM((2, 1, BLOCK), F32),
            pltpu.VMEM((n_z, 16, BLOCK), BF16),
            pltpu.VMEM((n_z, 1, BLOCK), F32),
            pltpu.VMEM((2, 16, BLOCK), F32),
            dma((6,)),
            dma((REACH,)),
            dma((2, REACH - 1)),
            dma((2, NFEAT)),
            dma((2, NFEAT)),
            dma((2, REACH)),
            dma((2, 2)),
            dma((2, 2)),
            dma((2, n_z)),
            dma((2, n_z)),
            dma((2, 2)),
            pltpu.SemaphoreType.REGULAR((2,)),
        ],
        compiler_params=pltpu.CompilerParams(
            collective_id=0, has_side_effects=True, vmem_limit_bytes=limit
        ),
        name="graph_layer",
    )(
        *(
            x if x is tile_counts else pltpu.with_memory_space_constraint(x, pltpu.HBM)
            for x in (
                node_features,
                weight.T,
                bias.reshape(1, HID_DEV),
                tile_values.reshape(PER_OFFSET, REACH, BLOCK, BLOCK),
                tile_src,
                tile_dst,
                tile_counts,
                out_grad.T,
            )
        )
    )
    out, wg, bg, ig = pl.pallas_call(
        finish,
        out_shape=shapes,
        in_specs=[anywhere] * 4,
        out_specs=(hbm,) * 4,
        scratch_shapes=[dma((4,))],
        compiler_params=pltpu.CompilerParams(vmem_limit_bytes=1024 * 1024),
        name="store_outputs",
    )(*results)
    return out.T, wg.T, bg.reshape(HID_DEV), ig.T


def solution(mesh):
    return jax.shard_map(
        shards,
        mesh=mesh,
        in_specs=(
            P("dom", None),
            P(None, "feat"),
            P("feat"),
            P("dom", None, None),
            P("dom"),
            P("dom"),
            P("dom"),
            P("dom", "feat"),
        ),
        out_specs=(P("dom", "feat"), P(None, "feat"), P("feat"), P("dom", "feat")),
        check_vma=False,
    )
```

```python
import functools

import jax
import jax.numpy as jnp
from jax import lax
from jax.experimental import pallas as pl
from jax.experimental.pallas import tpu as pltpu
from jax.sharding import PartitionSpec as P

REACH = 4
NB = 8
BLOCK = 128
NFEAT = 8
FW = 16
PER_OFFSET = 24
HID_DEV = 32
GROUP = 4
MESH = pl.DeviceIdType.MESH
F32 = jnp.float32
BF16 = jnp.bfloat16
ORDER = (3, 2, 1, 0)
HOPS = ((2, 1), (1, 1), (3, 1), (2, 0), (1, 0), (3, 0), (0, 1))


def kernel(
    n_dom,
    nf_hbm, wt_hbm, bias_hbm, tiles_hbm, src_hbm, dst_hbm, cnt, og_hbm,
    out, wg, bg, ig,
    nf, og, wt, bias, src, dst, tiles, nft, table, psend, precv, agg, hsend, hrecv,
    hall0, hall1, hall2, hall3,
    rsend, rrecv, rbias, zbuf, zbias, gbuf, gbias,
    load_sem, tile_sem, p_sem, a_sem, h_sem, b_sem, r_sem, z_sem, zb_sem, g_sem, gb_sem,
    relay_sem,
):
    n_z = n_dom // GROUP
    hall = (hall0, hall1, hall2, hall3)
    dom = lax.axis_index("dom")
    feat = lax.axis_index("feat")
    z = dom // GROUP
    lane = lax.rem(dom, GROUP)
    core = lax.rem(dom, 2)
    partner = (dom + 1 - 2 * core, feat)

    def dom_at(step):
        return lax.rem(dom + (step % n_dom), n_dom)

    def feat_at(hop):
        return lax.rem(feat // 2 + hop[0], NFEAT // 2) * 2 + lax.rem(feat + hop[1], 2)

    def z_at(step):
        return lax.rem(z + step, n_z)

    def z_peer(step):
        return (z_at(step) * GROUP + lane, feat)

    def group_peer(step):
        return (z * GROUP + lax.rem(lane + step, GROUP), feat)

    def around(*distances):
        return sorted({d % n_z for r in distances for d in (r, -r)} - {0})

    barrier = pltpu.get_barrier_semaphore()

    def signal(sem, device):
        pl.semaphore_signal(sem, inc=1, device_id=device, device_id_type=MESH)

    near = [(dom_at(step), feat) for step in range(1, REACH)]
    near += [(dom_at(-step), feat) for step in range(1, REACH)]
    near += [(dom, feat_at(hop)) for hop in HOPS]
    near += [z_peer(step) for step in around(1, 2)]
    for device in near:
        signal(barrier, device)

    pairs = [
        (src_hbm, src), (dst_hbm, dst), (nf_hbm, nf),
        (wt_hbm, wt), (bias_hbm, bias), (og_hbm, og),
    ]
    loads = [pltpu.make_async_copy(a, b, load_sem.at[i]) for i, (a, b) in enumerate(pairs)]
    tile_loads = [
        pltpu.make_async_copy(tiles_hbm.at[:, o], tiles.at[o], tile_sem.at[o])
        for o in range(REACH)
    ]
    for load in loads[:3]:
        load.start()
    for o in ORDER:
        tile_loads[o].start()
    for load in loads[3:]:
        load.start()

    sends = []

    def send(src_ref, dst_ref, sems, s, r, device):
        copy = pltpu.make_async_remote_copy(
            src_ref=src_ref,
            dst_ref=dst_ref,
            send_sem=sems.at[0, s],
            recv_sem=sems.at[1, r],
            device_id=device,
            device_id_type=MESH,
        )
        copy.start()
        sends.append(copy)

    def arrival(ref, sems, r):
        pltpu.make_async_copy(ref, ref, sems.at[1, r]).wait()

    one = jnp.ones((FW, BLOCK), BF16)
    zero = jnp.zeros((FW, BLOCK), BF16)
    for g in range(NB + 1):
        for row in range(NB):
            table[g, row * FW : (row + 1) * FW, :] = one if row == g else zero

    rows = lax.broadcasted_iota(jnp.int32, (FW, BLOCK), 0)
    columns = lax.broadcasted_iota(jnp.int32, (FW, BLOCK), 1)
    pick = jnp.where(columns == rows + feat * FW, 1.0, 0.0).astype(BF16)
    for load in loads[:3]:
        load.wait()
    picked = lax.dot_general(
        pick, nf[...], (((1,), (1,)), ((), ())), preferred_element_type=F32
    ).astype(BF16)
    for b in range(NB):
        nft[b] = picked[:, b * BLOCK : (b + 1) * BLOCK]

    used = cnt[0]

    def placed(block, position, k):
        position = jnp.where(k < used, position, NB)
        return jnp.concatenate([block] * NB, axis=0) * table[position]

    def forward(o):
        left = []
        right = []
        for j in range(PER_OFFSET):
            k = j * REACH + o
            left.append(placed(nft[src[k]], dst[k] & (NB - 1), k))
            right.append(tiles[o, j])
        return lax.dot_general(
            jnp.concatenate(left, axis=1),
            jnp.concatenate(right, axis=1),
            (((1,), (1,)), ((), ())),
            preferred_element_type=F32,
        )

    for o in ORDER[:-1]:
        tile_loads[o].wait()
        psend[o - 1] = forward(o).astype(BF16)
    pl.semaphore_wait(barrier, len(near))
    for o in ORDER[:-1]:
        send(psend.at[o - 1], precv.at[o - 1], p_sem, o - 1, o - 1, (dom_at(o), feat))
    for step in around(2):
        signal(relay_sem.at[0], z_peer(step))
    tile_loads[0].wait()
    own = forward(0)
    for load in loads[3:]:
        load.wait()
    bias_square = jnp.broadcast_to(bias[...], (HID_DEV, HID_DEV))
    on_diagonal = lax.broadcasted_iota(jnp.int32, (HID_DEV, HID_DEV), 0) == (
        lax.broadcasted_iota(jnp.int32, (HID_DEV, HID_DEV), 1)
    )
    bias_column = jnp.sum(jnp.where(on_diagonal, bias_square, 0.0), axis=1, keepdims=True)
    for o in ORDER[:-1]:
        arrival(precv.at[o - 1], p_sem, o - 1)
        own = own + precv[o - 1].astype(F32)
    agg[feat] = own.astype(BF16)
    for i, hop in enumerate(HOPS):
        send(agg.at[feat], agg.at[feat], a_sem, i, feat, (dom, feat_at(hop)))
    if around(2):
        pl.semaphore_wait(relay_sem.at[0], len(around(2)))
    for step in around(4):
        signal(relay_sem.at[1], z_peer(step))
    for hop in HOPS:
        arrival(agg.at[feat_at(hop)], a_sem, feat_at(hop))
    aggregated = jnp.concatenate(
        [
            jnp.concatenate([agg[i, g * FW : (g + 1) * FW, :] for i in range(NFEAT)], axis=0)
            for g in range(NB)
        ],
        axis=1,
    )
    pre = jnp.dot(wt[...], aggregated, preferred_element_type=F32) + bias_column
    sigmoid_pre = jax.nn.sigmoid(pre)
    grad_pre = (
        og[...].astype(F32) * sigmoid_pre * (1.0 + pre * (1.0 - sigmoid_pre))
    ).astype(BF16)

    weight_part = lax.dot_general(
        grad_pre, aggregated, (((1,), (1,)), ((), ())), preferred_element_type=F32
    )
    bias_part = lax.dot_general(
        jnp.ones((8, NB * BLOCK), BF16),
        jnp.concatenate([grad_pre] * 4, axis=0),
        (((1,), (1,)), ((), ())),
        preferred_element_type=F32,
    )
    rsend[0] = weight_part[0:16, :]
    rsend[1] = weight_part[16:32, :]
    rbias[0] = bias_part[0:1, :]
    send(rsend.at[1 - core], rrecv, r_sem, 0, 0, partner)
    send(rbias.at[0], rbias.at[1], r_sem, 1, 1, partner)

    back = lax.dot_general(
        wt[...], grad_pre, (((0,), (0,)), ((), ())), preferred_element_type=F32
    ).astype(BF16)
    for i in range(NFEAT):
        for g in range(NB):
            hsend[i, g * FW : (g + 1) * FW, :] = back[
                i * FW : (i + 1) * FW, g * BLOCK : (g + 1) * BLOCK
            ]
    for i, hop in enumerate(HOPS):
        send(hsend.at[feat_at(hop)], hrecv.at[feat], h_sem, i, feat, (dom, feat_at(hop)))
    hrecv[feat] = hsend[feat]

    if around(4):
        pl.semaphore_wait(relay_sem.at[1], len(around(4)))
    arrival(rrecv, r_sem, 0)
    arrival(rbias.at[1], r_sem, 1)
    zbuf[z] = (rsend[core] + rrecv[...]).astype(BF16)
    zbias[z] = rbias[0] + rbias[1]
    far_first = sorted(range(1, n_z), key=lambda step: -min(step, n_z - step))
    for step in far_first:
        send(zbuf.at[z], zbuf.at[z], z_sem, step, z, z_peer(step))
        send(zbias.at[z], zbias.at[z], zb_sem, step, z, z_peer(step))
    out[...] = (pre * sigmoid_pre).astype(BF16)

    for hop in HOPS:
        arrival(hrecv.at[feat_at(hop)], h_sem, feat_at(hop))
    mixed = hrecv[0].astype(F32)
    for i in range(1, NFEAT):
        mixed = mixed + hrecv[i].astype(F32)
    mixed = mixed.astype(BF16)
    for g in range(NB):
        hall0[g] = mixed[g * FW : (g + 1) * FW, :]
    for o in ORDER[:-1]:
        send(hall0, hall[o], b_sem, o, o, (dom_at(-o), feat))

    def backward(o):
        left = []
        for j in range(PER_OFFSET):
            k = j * REACH + o
            left.append(placed(hall[o][dst[k] & (NB - 1)], src[k], k))
        return jnp.dot(
            jnp.concatenate(left, axis=1),
            tiles[o].reshape(PER_OFFSET * BLOCK, BLOCK),
            preferred_element_type=F32,
        )

    total = backward(0)
    for step in far_first[::-1]:
        arrival(zbuf.at[z_at(step)], z_sem, z_at(step))
    gbuf[lane] = jnp.sum(zbuf[...].astype(F32), axis=0)
    for step in range(1, GROUP):
        send(gbuf.at[lane], gbuf.at[lane], g_sem, step, lane, group_peer(step))
    for step in far_first[::-1]:
        arrival(zbias.at[z_at(step)], zb_sem, z_at(step))
    gbias[lane] = jnp.sum(zbias[...], axis=0)
    for step in range(1, GROUP):
        send(gbias.at[lane], gbias.at[lane], gb_sem, step, lane, group_peer(step))
    for o in (1, 2, 3):
        arrival(hall[o], b_sem, o)
        total = total + backward(o)
    total = total.astype(BF16)
    for g in range(NB):
        ig[:, g * BLOCK : (g + 1) * BLOCK] = total[g * FW : (g + 1) * FW, :]

    for step in range(1, GROUP):
        member = lax.rem(lane + step, GROUP)
        arrival(gbuf.at[member], g_sem, member)
        arrival(gbias.at[member], gb_sem, member)
    wg[0:16, :] = gbuf[0] + gbuf[2]
    wg[16:32, :] = gbuf[1] + gbuf[3]
    bg[...] = (gbias[0] + gbias[2])[:, 0:HID_DEV]
    for copy in sends:
        copy.wait_send()


def finish(*refs):
    values, outs, sem = refs[:4], refs[4:8], refs[8]
    copies = [pltpu.make_async_copy(a, b, sem.at[i]) for i, (a, b) in enumerate(zip(values, outs))]
    for copy in copies:
        copy.start()
    for copy in copies:
        copy.wait()


def shards(node_features, weight, bias, tile_values, tile_src, tile_dst, tile_counts, out_grad):
    n_dom = lax.axis_size("dom")
    n_z = n_dom // GROUP
    nodes = NB * BLOCK
    vmem = pl.BlockSpec(memory_space=pltpu.VMEM)
    hbm = pl.BlockSpec(memory_space=pltpu.HBM)
    anywhere = pl.BlockSpec(memory_space=pl.ANY)
    dma = pltpu.SemaphoreType.DMA
    block = pltpu.VMEM((NB, FW, BLOCK), BF16)
    square = pltpu.VMEM((NFEAT, BLOCK, BLOCK), BF16)
    limit = 24 * 1024 * 1024
    shapes = (
        jax.ShapeDtypeStruct((HID_DEV, nodes), BF16),
        jax.ShapeDtypeStruct((HID_DEV, BLOCK), F32),
        jax.ShapeDtypeStruct((1, HID_DEV), F32),
        jax.ShapeDtypeStruct((FW, nodes), BF16),
    )
    results = pl.pallas_call(
        functools.partial(kernel, n_dom),
        out_shape=shapes,
        in_specs=[hbm] * 6 + [pl.BlockSpec(memory_space=pltpu.SMEM), hbm],
        out_specs=(vmem,) * 4,
        scratch_shapes=[
            pltpu.VMEM((nodes, BLOCK), BF16),
            pltpu.VMEM((HID_DEV, nodes), BF16),
            pltpu.VMEM((HID_DEV, BLOCK), BF16),
            pltpu.VMEM((1, HID_DEV), F32),
            pltpu.SMEM((PER_OFFSET * REACH,), jnp.int32),
            pltpu.SMEM((PER_OFFSET * REACH,), jnp.int32),
            pltpu.VMEM((REACH, PER_OFFSET, BLOCK, BLOCK), BF16),
            block,
            pltpu.VMEM((NB + 1, BLOCK, BLOCK), BF16),
            pltpu.VMEM((REACH - 1, BLOCK, BLOCK), BF16),
            pltpu.VMEM((REACH - 1, BLOCK, BLOCK), BF16),
            square,
            square,
            square,
            block,
            block,
            block,
            block,
            pltpu.VMEM((2, 16, BLOCK), F32),
            pltpu.VMEM((16, BLOCK), F32),
            pltpu.VMEM((2, 1, BLOCK), F32),
            pltpu.VMEM((n_z, 16, BLOCK), BF16),
            pltpu.VMEM((n_z, 1, BLOCK), F32),
            pltpu.VMEM((GROUP, 16, BLOCK), F32),
            pltpu.VMEM((GROUP, 1, BLOCK), F32),
            dma((6,)),
            dma((REACH,)),
            dma((2, REACH - 1)),
            dma((2, NFEAT)),
            dma((2, NFEAT)),
            dma((2, REACH)),
            dma((2, 2)),
            dma((2, n_z)),
            dma((2, n_z)),
            dma((2, GROUP)),
            dma((2, GROUP)),
            pltpu.SemaphoreType.REGULAR((2,)),
        ],
        compiler_params=pltpu.CompilerParams(
            collective_id=0, has_side_effects=True, vmem_limit_bytes=limit
        ),
        name="graph_layer",
    )(
        *(
            x if x is tile_counts else pltpu.with_memory_space_constraint(x, pltpu.HBM)
            for x in (
                node_features,
                weight.T,
                bias.reshape(1, HID_DEV),
                tile_values.reshape(PER_OFFSET, REACH, BLOCK, BLOCK),
                tile_src,
                tile_dst,
                tile_counts,
                out_grad.T,
            )
        )
    )
    out, wg, bg, ig = pl.pallas_call(
        finish,
        out_shape=shapes,
        in_specs=[anywhere] * 4,
        out_specs=(hbm,) * 4,
        scratch_shapes=[dma((4,))],
        compiler_params=pltpu.CompilerParams(vmem_limit_bytes=1024 * 1024),
        name="store_outputs",
    )(*results)
    return out.T, wg.T, bg.reshape(HID_DEV), ig.T


def solution(mesh):
    return jax.shard_map(
        shards,
        mesh=mesh,
        in_specs=(
            P("dom", None),
            P(None, "feat"),
            P("feat"),
            P("dom", None, None),
            P("dom"),
            P("dom"),
            P("dom"),
            P("dom", "feat"),
        ),
        out_specs=(P("dom", "feat"), P(None, "feat"), P("feat"), P("dom", "feat")),
        check_vma=False,
    )
```

```python
import functools

import jax
import jax.numpy as jnp
from jax import lax
from jax.experimental import pallas as pl
from jax.experimental.pallas import tpu as pltpu
from jax.sharding import PartitionSpec as P

REACH = 4
NB = 8
BLOCK = 128
NFEAT = 8
FW = 16
PER_OFFSET = 24
HID_DEV = 32
GROUP = 4
MESH = pl.DeviceIdType.MESH
F32 = jnp.float32
BF16 = jnp.bfloat16
ORDER = (3, 2, 1, 0)
HOPS = ((2, 1), (1, 1), (3, 1), (2, 0), (1, 0), (3, 0), (0, 1))


def kernel(
    n_dom,
    nf_hbm, wt_hbm, bias_hbm, tiles_hbm, src_hbm, dst_hbm, cnt, og_hbm,
    out, wg, bg, ig,
    nf, og, wt, bias, src, dst, tiles, nft, table, psend, precv, agg, hsend, hrecv,
    hall0, hall1, hall2, hall3,
    rsend, rrecv, rbias, zbuf, zbias, gbuf, gbias,
    load_sem, tile_sem, p_sem, a_sem, h_sem, b_sem, r_sem, rb_sem, z_sem, zb_sem, g_sem, gb_sem,
    relay_sem,
):
    n_z = n_dom // GROUP
    hall = (hall0, hall1, hall2, hall3)
    dom = lax.axis_index("dom")
    feat = lax.axis_index("feat")
    z = dom // GROUP
    lane = lax.rem(dom, GROUP)
    core = lax.rem(dom, 2)
    partner = (dom + 1 - 2 * core, feat)

    def dom_at(step):
        return lax.rem(dom + (step % n_dom), n_dom)

    def feat_at(hop):
        return lax.rem(feat // 2 + hop[0], NFEAT // 2) * 2 + lax.rem(feat + hop[1], 2)

    def z_at(step):
        return lax.rem(z + step, n_z)

    def z_peer(step):
        return (z_at(step) * GROUP + lane, feat)

    def group_peer(step):
        return (z * GROUP + lax.rem(lane + step, GROUP), feat)

    def around(*distances):
        return sorted({d % n_z for r in distances for d in (r, -r)} - {0})

    barrier = pltpu.get_barrier_semaphore()

    def signal(sem, device):
        pl.semaphore_signal(sem, inc=1, device_id=device, device_id_type=MESH)

    near = [(dom_at(step), feat) for step in range(1, REACH)]
    near += [(dom_at(-step), feat) for step in range(1, REACH)]
    near += [(dom, feat_at(hop)) for hop in HOPS]
    near += [z_peer(step) for step in around(1, 2)]
    for device in near:
        signal(barrier, device)

    pairs = [
        (src_hbm, src), (dst_hbm, dst), (nf_hbm, nf),
        (wt_hbm, wt), (bias_hbm, bias), (og_hbm, og),
    ]
    loads = [pltpu.make_async_copy(a, b, load_sem.at[i]) for i, (a, b) in enumerate(pairs)]
    tile_loads = [
        pltpu.make_async_copy(tiles_hbm.at[:, o], tiles.at[o], tile_sem.at[o])
        for o in range(REACH)
    ]
    for load in loads[:3]:
        load.start()
    for o in ORDER:
        tile_loads[o].start()
    for load in loads[3:]:
        load.start()

    def send(src_ref, dst_ref, sems, device, r=1):
        pltpu.make_async_remote_copy(
            src_ref=src_ref,
            dst_ref=dst_ref,
            send_sem=sems.at[0],
            recv_sem=sems.at[r],
            device_id=device,
            device_id_type=MESH,
        ).start()

    def sent(ref, sems):
        pltpu.make_async_copy(ref, ref, sems.at[0]).wait()

    def arrival(ref, sems, r=1):
        pltpu.make_async_copy(ref, ref, sems.at[r]).wait()

    one = jnp.ones((FW, BLOCK), BF16)
    zero = jnp.zeros((FW, BLOCK), BF16)
    for g in range(NB + 1):
        for row in range(NB):
            table[g, row * FW : (row + 1) * FW, :] = one if row == g else zero

    rows = lax.broadcasted_iota(jnp.int32, (FW, BLOCK), 0)
    columns = lax.broadcasted_iota(jnp.int32, (FW, BLOCK), 1)
    pick = jnp.where(columns == rows + feat * FW, 1.0, 0.0).astype(BF16)
    for load in loads[:3]:
        load.wait()
    picked = lax.dot_general(
        pick, nf[...], (((1,), (1,)), ((), ())), preferred_element_type=F32
    ).astype(BF16)
    for b in range(NB):
        nft[b] = picked[:, b * BLOCK : (b + 1) * BLOCK]

    used = cnt[0]

    def placed(block, position, k):
        position = jnp.where(k < used, position, NB)
        return jnp.concatenate([block] * NB, axis=0) * table[position]

    def forward(o):
        left = []
        right = []
        for j in range(PER_OFFSET):
            k = j * REACH + o
            left.append(placed(nft[src[k]], dst[k] & (NB - 1), k))
            right.append(tiles[o, j])
        return lax.dot_general(
            jnp.concatenate(left, axis=1),
            jnp.concatenate(right, axis=1),
            (((1,), (1,)), ((), ())),
            preferred_element_type=F32,
        )

    for o in ORDER[:-1]:
        tile_loads[o].wait()
        psend[o - 1] = forward(o).astype(BF16)
    pl.semaphore_wait(barrier, len(near))
    for o in ORDER[:-1]:
        send(psend.at[o - 1], precv.at[o - 1], p_sem, (dom_at(o), feat))
    for step in around(2):
        signal(relay_sem.at[0], z_peer(step))
    tile_loads[0].wait()
    own = forward(0)
    for load in loads[3:]:
        load.wait()
    bias_square = jnp.broadcast_to(bias[...], (HID_DEV, HID_DEV))
    on_diagonal = lax.broadcasted_iota(jnp.int32, (HID_DEV, HID_DEV), 0) == (
        lax.broadcasted_iota(jnp.int32, (HID_DEV, HID_DEV), 1)
    )
    bias_column = jnp.sum(jnp.where(on_diagonal, bias_square, 0.0), axis=1, keepdims=True)
    arrival(precv, p_sem)
    for o in ORDER[:-1]:
        own = own + precv[o - 1].astype(F32)
    agg[feat] = own.astype(BF16)
    for hop in HOPS:
        send(agg.at[feat], agg.at[feat], a_sem, (dom, feat_at(hop)))
    if around(2):
        pl.semaphore_wait(relay_sem.at[0], len(around(2)))
    for step in around(4):
        signal(relay_sem.at[1], z_peer(step))
    arrival(agg.at[0 : NFEAT - 1], a_sem)
    aggregated = jnp.concatenate(
        [
            jnp.concatenate([agg[i, g * FW : (g + 1) * FW, :] for i in range(NFEAT)], axis=0)
            for g in range(NB)
        ],
        axis=1,
    )
    pre = jnp.dot(wt[...], aggregated, preferred_element_type=F32) + bias_column
    sigmoid_pre = jax.nn.sigmoid(pre)
    grad_pre = (
        og[...].astype(F32) * sigmoid_pre * (1.0 + pre * (1.0 - sigmoid_pre))
    ).astype(BF16)

    weight_part = lax.dot_general(
        grad_pre, aggregated, (((1,), (1,)), ((), ())), preferred_element_type=F32
    )
    bias_part = lax.dot_general(
        jnp.ones((8, NB * BLOCK), BF16),
        jnp.concatenate([grad_pre] * 4, axis=0),
        (((1,), (1,)), ((), ())),
        preferred_element_type=F32,
    )
    rsend[0] = weight_part[0:16, :]
    rsend[1] = weight_part[16:32, :]
    rbias[0] = bias_part[0:1, :]
    send(rsend.at[1 - core], rrecv, r_sem, partner)
    send(rbias.at[0], rbias.at[1], rb_sem, partner)

    back = lax.dot_general(
        wt[...], grad_pre, (((0,), (0,)), ((), ())), preferred_element_type=F32
    ).astype(BF16)
    for i in range(NFEAT):
        for g in range(NB):
            hsend[i, g * FW : (g + 1) * FW, :] = back[
                i * FW : (i + 1) * FW, g * BLOCK : (g + 1) * BLOCK
            ]
    for hop in HOPS:
        send(hsend.at[feat_at(hop)], hrecv.at[feat], h_sem, (dom, feat_at(hop)))
    hrecv[feat] = hsend[feat]

    if around(4):
        pl.semaphore_wait(relay_sem.at[1], len(around(4)))
    arrival(rrecv, r_sem)
    arrival(rbias.at[1], rb_sem)
    zbuf[z] = (rsend[core] + rrecv[...]).astype(BF16)
    zbias[z] = rbias[0] + rbias[1]
    far_first = sorted(range(1, n_z), key=lambda step: -min(step, n_z - step))
    for step in far_first:
        send(zbuf.at[z], zbuf.at[z], z_sem, z_peer(step))
        send(zbias.at[z], zbias.at[z], zb_sem, z_peer(step))
    out[...] = (pre * sigmoid_pre).astype(BF16)

    arrival(hrecv.at[0 : NFEAT - 1], h_sem)
    mixed = hrecv[0].astype(F32)
    for i in range(1, NFEAT):
        mixed = mixed + hrecv[i].astype(F32)
    mixed = mixed.astype(BF16)
    for g in range(NB):
        hall0[g] = mixed[g * FW : (g + 1) * FW, :]
    for o in ORDER[:-1]:
        send(hall0, hall[o], b_sem, (dom_at(-o), feat), o)

    def backward(o):
        left = []
        for j in range(PER_OFFSET):
            k = j * REACH + o
            left.append(placed(hall[o][dst[k] & (NB - 1)], src[k], k))
        return jnp.dot(
            jnp.concatenate(left, axis=1),
            tiles[o].reshape(PER_OFFSET * BLOCK, BLOCK),
            preferred_element_type=F32,
        )

    total = backward(0)
    arrival(zbuf.at[0 : n_z - 1], z_sem)
    gbuf[lane] = jnp.sum(zbuf[...].astype(F32), axis=0)
    for step in range(1, GROUP):
        send(gbuf.at[lane], gbuf.at[lane], g_sem, group_peer(step))
    arrival(zbias.at[0 : n_z - 1], zb_sem)
    gbias[lane] = jnp.sum(zbias[...], axis=0)
    for step in range(1, GROUP):
        send(gbias.at[lane], gbias.at[lane], gb_sem, group_peer(step))
    for o in (1, 2, 3):
        arrival(hall[o], b_sem, o)
        total = total + backward(o)
    total = total.astype(BF16)
    for g in range(NB):
        ig[:, g * BLOCK : (g + 1) * BLOCK] = total[g * FW : (g + 1) * FW, :]

    arrival(gbuf.at[0 : GROUP - 1], g_sem)
    arrival(gbias.at[0 : GROUP - 1], gb_sem)
    wg[0:16, :] = gbuf[0] + gbuf[2]
    wg[16:32, :] = gbuf[1] + gbuf[3]
    bg[...] = (gbias[0] + gbias[2])[:, 0:HID_DEV]
    sent(psend, p_sem)
    sent(agg.at[0 : NFEAT - 1], a_sem)
    sent(rsend.at[0], r_sem)
    sent(rbias.at[0], rb_sem)
    sent(hsend.at[0 : NFEAT - 1], h_sem)
    sent(zbuf.at[0 : n_z - 1], z_sem)
    sent(zbias.at[0 : n_z - 1], zb_sem)
    sent(psend, b_sem)
    sent(gbuf.at[0 : GROUP - 1], g_sem)
    sent(gbias.at[0 : GROUP - 1], gb_sem)


def finish(*refs):
    values, outs, sem = refs[:4], refs[4:8], refs[8]
    copies = [pltpu.make_async_copy(a, b, sem.at[i]) for i, (a, b) in enumerate(zip(values, outs))]
    for copy in copies:
        copy.start()
    for copy in copies:
        copy.wait()


def shards(node_features, weight, bias, tile_values, tile_src, tile_dst, tile_counts, out_grad):
    n_dom = lax.axis_size("dom")
    n_z = n_dom // GROUP
    nodes = NB * BLOCK
    vmem = pl.BlockSpec(memory_space=pltpu.VMEM)
    hbm = pl.BlockSpec(memory_space=pltpu.HBM)
    anywhere = pl.BlockSpec(memory_space=pl.ANY)
    dma = pltpu.SemaphoreType.DMA
    block = pltpu.VMEM((NB, FW, BLOCK), BF16)
    square = pltpu.VMEM((NFEAT, BLOCK, BLOCK), BF16)
    limit = 24 * 1024 * 1024
    shapes = (
        jax.ShapeDtypeStruct((HID_DEV, nodes), BF16),
        jax.ShapeDtypeStruct((HID_DEV, BLOCK), F32),
        jax.ShapeDtypeStruct((1, HID_DEV), F32),
        jax.ShapeDtypeStruct((FW, nodes), BF16),
    )
    results = pl.pallas_call(
        functools.partial(kernel, n_dom),
        out_shape=shapes,
        in_specs=[hbm] * 6 + [pl.BlockSpec(memory_space=pltpu.SMEM), hbm],
        out_specs=(vmem,) * 4,
        scratch_shapes=[
            pltpu.VMEM((nodes, BLOCK), BF16),
            pltpu.VMEM((HID_DEV, nodes), BF16),
            pltpu.VMEM((HID_DEV, BLOCK), BF16),
            pltpu.VMEM((1, HID_DEV), F32),
            pltpu.SMEM((PER_OFFSET * REACH,), jnp.int32),
            pltpu.SMEM((PER_OFFSET * REACH,), jnp.int32),
            pltpu.VMEM((REACH, PER_OFFSET, BLOCK, BLOCK), BF16),
            block,
            pltpu.VMEM((NB + 1, BLOCK, BLOCK), BF16),
            pltpu.VMEM((REACH - 1, BLOCK, BLOCK), BF16),
            pltpu.VMEM((REACH - 1, BLOCK, BLOCK), BF16),
            square,
            square,
            square,
            block,
            block,
            block,
            block,
            pltpu.VMEM((2, 16, BLOCK), F32),
            pltpu.VMEM((16, BLOCK), F32),
            pltpu.VMEM((2, 1, BLOCK), F32),
            pltpu.VMEM((n_z, 16, BLOCK), BF16),
            pltpu.VMEM((n_z, 1, BLOCK), F32),
            pltpu.VMEM((GROUP, 16, BLOCK), F32),
            pltpu.VMEM((GROUP, 1, BLOCK), F32),
            dma((6,)),
            dma((REACH,)),
            dma((2,)),
            dma((2,)),
            dma((2,)),
            dma((REACH,)),
            dma((2,)),
            dma((2,)),
            dma((2,)),
            dma((2,)),
            dma((2,)),
            dma((2,)),
            pltpu.SemaphoreType.REGULAR((2,)),
        ],
        compiler_params=pltpu.CompilerParams(
            collective_id=0, has_side_effects=True, vmem_limit_bytes=limit
        ),
        name="graph_layer",
    )(
        *(
            x if x is tile_counts else pltpu.with_memory_space_constraint(x, pltpu.HBM)
            for x in (
                node_features,
                weight.T,
                bias.reshape(1, HID_DEV),
                tile_values.reshape(PER_OFFSET, REACH, BLOCK, BLOCK),
                tile_src,
                tile_dst,
                tile_counts,
                out_grad.T,
            )
        )
    )
    out, wg, bg, ig = pl.pallas_call(
        finish,
        out_shape=shapes,
        in_specs=[anywhere] * 4,
        out_specs=(hbm,) * 4,
        scratch_shapes=[dma((4,))],
        compiler_params=pltpu.CompilerParams(vmem_limit_bytes=1024 * 1024),
        name="store_outputs",
    )(*results)
    return out.T, wg.T, bg.reshape(HID_DEV), ig.T


def solution(mesh):
    return jax.shard_map(
        shards,
        mesh=mesh,
        in_specs=(
            P("dom", None),
            P(None, "feat"),
            P("feat"),
            P("dom", None, None),
            P("dom"),
            P("dom"),
            P("dom"),
            P("dom", "feat"),
        ),
        out_specs=(P("dom", "feat"), P(None, "feat"), P("feat"), P("dom", "feat")),
        check_vma=False,
    )
```

```python
import functools

import jax
import jax.numpy as jnp
from jax import lax
from jax.experimental import pallas as pl
from jax.experimental.pallas import tpu as pltpu
from jax.sharding import PartitionSpec as P

REACH = 4
NB = 8
BLOCK = 128
NFEAT = 8
FW = 16
PER_OFFSET = 24
HALVES = (0, 1)
HALF = 64
HID_DEV = 32
GROUP = 4
MESH = pl.DeviceIdType.MESH
F32 = jnp.float32
BF16 = jnp.bfloat16
ORDER = (3, 2, 1, 0)
HOPS = ((2, 1), (1, 1), (3, 1), (2, 0), (1, 0), (3, 0), (0, 1))


def kernel(
    n_dom,
    nf_hbm, wt_hbm, bias_hbm, tiles_hbm, src_hbm, dst_hbm, cnt, og_hbm,
    out, wg, bg, ig,
    nf, og, wt, bias, src, dst, tiles, nft, table, psend, precv, agg, hsend, hrecv,
    hall0, hall1, hall2, hall3,
    rsend, rrecv, rbias, zbuf, zbias, gbuf, gbias,
    load_sem, tile_sem, p_sem, a_sem, h_sem, b_sem, r_sem, rb_sem, z_sem, zb_sem, g_sem, gb_sem,
    relay_sem,
):
    n_z = n_dom // GROUP
    hall = (hall0, hall1, hall2, hall3)
    dom = lax.axis_index("dom")
    feat = lax.axis_index("feat")
    z = dom // GROUP
    lane = lax.rem(dom, GROUP)
    core = lax.rem(dom, 2)
    partner = (dom + 1 - 2 * core, feat)

    def dom_at(step):
        return lax.rem(dom + (step % n_dom), n_dom)

    def feat_at(hop):
        return lax.rem(feat // 2 + hop[0], NFEAT // 2) * 2 + lax.rem(feat + hop[1], 2)

    def z_at(step):
        return lax.rem(z + step, n_z)

    def z_peer(step):
        return (z_at(step) * GROUP + lane, feat)

    def group_peer(step):
        return (z * GROUP + lax.rem(lane + step, GROUP), feat)

    def around(*distances):
        return sorted({d % n_z for r in distances for d in (r, -r)} - {0})

    barrier = pltpu.get_barrier_semaphore()

    def signal(sem, device):
        pl.semaphore_signal(sem, inc=1, device_id=device, device_id_type=MESH)

    near = [(dom_at(step), feat) for step in range(1, REACH)]
    near += [(dom_at(-step), feat) for step in range(1, REACH)]
    near += [(dom, feat_at(hop)) for hop in HOPS]
    near += [z_peer(step) for step in around(1, 2)]
    for device in near:
        signal(barrier, device)

    pairs = [
        (src_hbm, src), (dst_hbm, dst), (nf_hbm, nf),
        (wt_hbm, wt), (bias_hbm, bias), (og_hbm, og),
    ]
    loads = [pltpu.make_async_copy(a, b, load_sem.at[i]) for i, (a, b) in enumerate(pairs)]
    tile_loads = [
        pltpu.make_async_copy(tiles_hbm.at[:, o], tiles.at[o], tile_sem.at[o])
        for o in range(REACH)
    ]
    for load in loads[:3]:
        load.start()
    for o in ORDER:
        tile_loads[o].start()
    for load in loads[3:]:
        load.start()

    def send(src_ref, dst_ref, sems, device, r=1):
        pltpu.make_async_remote_copy(
            src_ref=src_ref,
            dst_ref=dst_ref,
            send_sem=sems.at[0],
            recv_sem=sems.at[r],
            device_id=device,
            device_id_type=MESH,
        ).start()

    def sent(ref, sems):
        pltpu.make_async_copy(ref, ref, sems.at[0]).wait()

    def arrival(ref, sems, r=1):
        pltpu.make_async_copy(ref, ref, sems.at[r]).wait()

    one = jnp.ones((FW, BLOCK), BF16)
    zero = jnp.zeros((FW, BLOCK), BF16)
    for g in range(NB + 1):
        for row in range(NB):
            table[g, row * FW : (row + 1) * FW, :] = one if row == g else zero

    rows = lax.broadcasted_iota(jnp.int32, (FW, BLOCK), 0)
    columns = lax.broadcasted_iota(jnp.int32, (FW, BLOCK), 1)
    pick = jnp.where(columns == rows + feat * FW, 1.0, 0.0).astype(BF16)
    for load in loads[:3]:
        load.wait()
    picked = lax.dot_general(
        pick, nf[...], (((1,), (1,)), ((), ())), preferred_element_type=F32
    ).astype(BF16)
    for b in range(NB):
        nft[b] = picked[:, b * BLOCK : (b + 1) * BLOCK]

    used = cnt[0]

    def placed(block, position, k):
        position = jnp.where(k < used, position, NB)
        return jnp.concatenate([block] * NB, axis=0) * table[position]

    def forward(o):
        left = []
        right = []
        for j in range(PER_OFFSET):
            k = j * REACH + o
            left.append(placed(nft[src[k]], dst[k] & (NB - 1), k))
            right.append(tiles[o, j])
        return lax.dot_general(
            jnp.concatenate(left, axis=1),
            jnp.concatenate(right, axis=1),
            (((1,), (1,)), ((), ())),
            preferred_element_type=F32,
        )

    for o in ORDER[:-1]:
        tile_loads[o].wait()
        part = forward(o).astype(BF16)
        for half in HALVES:
            psend[half, o - 1] = part[half * HALF : (half + 1) * HALF, :]
    pl.semaphore_wait(barrier, len(near))
    for half in HALVES:
        for o in ORDER[:-1]:
            send(
                psend.at[half, o - 1], precv.at[half, o - 1], p_sem, (dom_at(o), feat), 1 + half
            )
    for step in around(2):
        signal(relay_sem.at[0], z_peer(step))
    tile_loads[0].wait()
    own = forward(0)
    for load in loads[3:]:
        load.wait()
    bias_square = jnp.broadcast_to(bias[...], (HID_DEV, HID_DEV))
    on_diagonal = lax.broadcasted_iota(jnp.int32, (HID_DEV, HID_DEV), 0) == (
        lax.broadcasted_iota(jnp.int32, (HID_DEV, HID_DEV), 1)
    )
    bias_column = jnp.sum(jnp.where(on_diagonal, bias_square, 0.0), axis=1, keepdims=True)
    for half in HALVES:
        arrival(precv.at[half], p_sem, 1 + half)
        piece = own[half * HALF : (half + 1) * HALF, :]
        for o in ORDER[:-1]:
            piece = piece + precv[half, o - 1].astype(F32)
        agg[half, feat] = piece.astype(BF16)
        for hop in HOPS:
            send(
                agg.at[half, feat], agg.at[half, feat], a_sem, (dom, feat_at(hop)), 1 + half
            )
    if around(2):
        pl.semaphore_wait(relay_sem.at[0], len(around(2)))
    for step in around(4):
        signal(relay_sem.at[1], z_peer(step))

    def send_back(grad_pre, half):
        back = lax.dot_general(
            wt[...], grad_pre, (((0,), (0,)), ((), ())), preferred_element_type=F32
        ).astype(BF16)
        for i in range(NFEAT):
            for g in range(NB // 2):
                hsend[half, i, g * FW : (g + 1) * FW, :] = back[
                    i * FW : (i + 1) * FW, g * BLOCK : (g + 1) * BLOCK
                ]
        for hop in HOPS:
            send(
                hsend.at[half, feat_at(hop)], hrecv.at[half, feat], h_sem,
                (dom, feat_at(hop)), 1 + half,
            )
        hrecv[half, feat] = hsend[half, feat]

    weight_part = jnp.zeros((HID_DEV, BLOCK), F32)
    bias_part = jnp.zeros((8, BLOCK), F32)
    for half in HALVES:
        arrival(agg.at[half, 0 : NFEAT - 1], a_sem, 1 + half)
        aggregated = jnp.concatenate(
            [
                jnp.concatenate(
                    [agg[half, i, g * FW : (g + 1) * FW, :] for i in range(NFEAT)], axis=0
                )
                for g in range(NB // 2)
            ],
            axis=1,
        )
        nodes = slice(half * NB // 2 * BLOCK, (half + 1) * NB // 2 * BLOCK)
        pre = jnp.dot(wt[...], aggregated, preferred_element_type=F32) + bias_column
        sigmoid_pre = jax.nn.sigmoid(pre)
        grad_pre = (
            og[:, nodes].astype(F32) * sigmoid_pre * (1.0 + pre * (1.0 - sigmoid_pre))
        ).astype(BF16)
        if half == 0:
            send_back(grad_pre, half)
        out[:, nodes] = (pre * sigmoid_pre).astype(BF16)
        weight_part = weight_part + lax.dot_general(
            grad_pre, aggregated, (((1,), (1,)), ((), ())), preferred_element_type=F32
        )
        bias_part = bias_part + lax.dot_general(
            jnp.ones((8, NB // 2 * BLOCK), BF16),
            jnp.concatenate([grad_pre] * 4, axis=0),
            (((1,), (1,)), ((), ())),
            preferred_element_type=F32,
        )
    rsend[0] = weight_part[0:16, :]
    rsend[1] = weight_part[16:32, :]
    rbias[0] = bias_part[0:1, :]
    send(rsend.at[1 - core], rrecv, r_sem, partner)
    send(rbias.at[0], rbias.at[1], rb_sem, partner)

    send_back(grad_pre, 1)

    if around(4):
        pl.semaphore_wait(relay_sem.at[1], len(around(4)))
    arrival(rrecv, r_sem)
    arrival(rbias.at[1], rb_sem)
    zbuf[z] = (rsend[core] + rrecv[...]).astype(BF16)
    zbias[z] = rbias[0] + rbias[1]
    far_first = sorted(range(1, n_z), key=lambda step: -min(step, n_z - step))
    for step in far_first:
        send(zbuf.at[z], zbuf.at[z], z_sem, z_peer(step))
        send(zbias.at[z], zbias.at[z], zb_sem, z_peer(step))

    for half in HALVES:
        arrival(hrecv.at[half, 0 : NFEAT - 1], h_sem, 1 + half)
        mixed = hrecv[half, 0].astype(F32)
        for i in range(1, NFEAT):
            mixed = mixed + hrecv[half, i].astype(F32)
        mixed = mixed.astype(BF16)
        first = half * NB // 2
        for g in range(NB // 2):
            hall0[first + g] = mixed[g * FW : (g + 1) * FW, :]
        blocks = pl.ds(first, NB // 2)
        for o in ORDER[:-1]:
            send(hall0.at[blocks], hall[o].at[blocks], b_sem, (dom_at(-o), feat), o)

    def backward(o):
        left = []
        for j in range(PER_OFFSET):
            k = j * REACH + o
            left.append(placed(hall[o][dst[k] & (NB - 1)], src[k], k))
        return jnp.dot(
            jnp.concatenate(left, axis=1),
            tiles[o].reshape(PER_OFFSET * BLOCK, BLOCK),
            preferred_element_type=F32,
        )

    total = backward(0)
    arrival(zbuf.at[0 : n_z - 1], z_sem)
    gbuf[lane] = jnp.sum(zbuf[...].astype(F32), axis=0)
    for step in range(1, GROUP):
        send(gbuf.at[lane], gbuf.at[lane], g_sem, group_peer(step))
    arrival(zbias.at[0 : n_z - 1], zb_sem)
    gbias[lane] = jnp.sum(zbias[...], axis=0)
    for step in range(1, GROUP):
        send(gbias.at[lane], gbias.at[lane], gb_sem, group_peer(step))
    for o in (1, 2, 3):
        arrival(hall[o], b_sem, o)
        total = total + backward(o)
    total = total.astype(BF16)
    for g in range(NB):
        ig[:, g * BLOCK : (g + 1) * BLOCK] = total[g * FW : (g + 1) * FW, :]

    arrival(gbuf.at[0 : GROUP - 1], g_sem)
    arrival(gbias.at[0 : GROUP - 1], gb_sem)
    wg[0:16, :] = gbuf[0] + gbuf[2]
    wg[16:32, :] = gbuf[1] + gbuf[3]
    bg[...] = (gbias[0] + gbias[2])[:, 0:HID_DEV]
    sent(psend, p_sem)
    sent(agg.at[:, 0 : NFEAT - 1], a_sem)
    sent(rsend.at[0], r_sem)
    sent(rbias.at[0], rb_sem)
    sent(hsend.at[:, 0 : NFEAT - 1], h_sem)
    sent(zbuf.at[0 : n_z - 1], z_sem)
    sent(zbias.at[0 : n_z - 1], zb_sem)
    sent(psend, b_sem)
    sent(gbuf.at[0 : GROUP - 1], g_sem)
    sent(gbias.at[0 : GROUP - 1], gb_sem)


def finish(*refs):
    values, outs, sem = refs[:4], refs[4:8], refs[8]
    copies = [pltpu.make_async_copy(a, b, sem.at[i]) for i, (a, b) in enumerate(zip(values, outs))]
    for copy in copies:
        copy.start()
    for copy in copies:
        copy.wait()


def shards(node_features, weight, bias, tile_values, tile_src, tile_dst, tile_counts, out_grad):
    n_dom = lax.axis_size("dom")
    n_z = n_dom // GROUP
    nodes = NB * BLOCK
    vmem = pl.BlockSpec(memory_space=pltpu.VMEM)
    hbm = pl.BlockSpec(memory_space=pltpu.HBM)
    anywhere = pl.BlockSpec(memory_space=pl.ANY)
    dma = pltpu.SemaphoreType.DMA
    block = pltpu.VMEM((NB, FW, BLOCK), BF16)
    square = pltpu.VMEM((2, NFEAT, HALF, BLOCK), BF16)
    limit = 24 * 1024 * 1024
    shapes = (
        jax.ShapeDtypeStruct((HID_DEV, nodes), BF16),
        jax.ShapeDtypeStruct((HID_DEV, BLOCK), F32),
        jax.ShapeDtypeStruct((1, HID_DEV), F32),
        jax.ShapeDtypeStruct((FW, nodes), BF16),
    )
    results = pl.pallas_call(
        functools.partial(kernel, n_dom),
        out_shape=shapes,
        in_specs=[hbm] * 6 + [pl.BlockSpec(memory_space=pltpu.SMEM), hbm],
        out_specs=(vmem,) * 4,
        scratch_shapes=[
            pltpu.VMEM((nodes, BLOCK), BF16),
            pltpu.VMEM((HID_DEV, nodes), BF16),
            pltpu.VMEM((HID_DEV, BLOCK), BF16),
            pltpu.VMEM((1, HID_DEV), F32),
            pltpu.SMEM((PER_OFFSET * REACH,), jnp.int32),
            pltpu.SMEM((PER_OFFSET * REACH,), jnp.int32),
            pltpu.VMEM((REACH, PER_OFFSET, BLOCK, BLOCK), BF16),
            block,
            pltpu.VMEM((NB + 1, BLOCK, BLOCK), BF16),
            pltpu.VMEM((2, REACH - 1, HALF, BLOCK), BF16),
            pltpu.VMEM((2, REACH - 1, HALF, BLOCK), BF16),
            square,
            square,
            square,
            block,
            block,
            block,
            block,
            pltpu.VMEM((2, 16, BLOCK), F32),
            pltpu.VMEM((16, BLOCK), F32),
            pltpu.VMEM((2, 1, BLOCK), F32),
            pltpu.VMEM((n_z, 16, BLOCK), BF16),
            pltpu.VMEM((n_z, 1, BLOCK), F32),
            pltpu.VMEM((GROUP, 16, BLOCK), F32),
            pltpu.VMEM((GROUP, 1, BLOCK), F32),
            dma((6,)),
            dma((REACH,)),
            dma((3,)),
            dma((3,)),
            dma((3,)),
            dma((REACH,)),
            dma((2,)),
            dma((2,)),
            dma((2,)),
            dma((2,)),
            dma((2,)),
            dma((2,)),
            pltpu.SemaphoreType.REGULAR((2,)),
        ],
        compiler_params=pltpu.CompilerParams(
            collective_id=0, has_side_effects=True, vmem_limit_bytes=limit
        ),
        name="graph_layer",
    )(
        *(
            x if x is tile_counts else pltpu.with_memory_space_constraint(x, pltpu.HBM)
            for x in (
                node_features,
                weight.T,
                bias.reshape(1, HID_DEV),
                tile_values.reshape(PER_OFFSET, REACH, BLOCK, BLOCK),
                tile_src,
                tile_dst,
                tile_counts,
                out_grad.T,
            )
        )
    )
    out, wg, bg, ig = pl.pallas_call(
        finish,
        out_shape=shapes,
        in_specs=[anywhere] * 4,
        out_specs=(hbm,) * 4,
        scratch_shapes=[dma((4,))],
        compiler_params=pltpu.CompilerParams(vmem_limit_bytes=1024 * 1024),
        name="store_outputs",
    )(*results)
    return out.T, wg.T, bg.reshape(HID_DEV), ig.T


def solution(mesh):
    return jax.shard_map(
        shards,
        mesh=mesh,
        in_specs=(
            P("dom", None),
            P(None, "feat"),
            P("feat"),
            P("dom", None, None),
            P("dom"),
            P("dom"),
            P("dom"),
            P("dom", "feat"),
        ),
        out_specs=(P("dom", "feat"), P(None, "feat"), P("feat"), P("dom", "feat")),
        check_vma=False,
    )
```

```python
import functools

import jax
import jax.numpy as jnp
from jax import lax
from jax.experimental import pallas as pl
from jax.experimental.pallas import tpu as pltpu
from jax.sharding import PartitionSpec as P

REACH = 4
NB = 8
BLOCK = 128
NFEAT = 8
FW = 16
PER_OFFSET = 24
PIECES = (0, 1, 2, 3)
ROWS = 32
SPAN = 2
HID_DEV = 32
GROUP = 4
MESH = pl.DeviceIdType.MESH
F32 = jnp.float32
BF16 = jnp.bfloat16
ORDER = (3, 2, 1, 0)
HOPS = ((2, 1), (1, 1), (3, 1), (2, 0), (1, 0), (3, 0), (0, 1))


def kernel(
    n_dom,
    nf_hbm, wt_hbm, bias_hbm, tiles_hbm, src_hbm, dst_hbm, cnt, og_hbm,
    out, wg, bg, ig,
    nf, og, wt, bias, src, dst, tiles, nft, table, psend, precv, agg, hsend, hrecv,
    hall0, hall1, hall2, hall3,
    rsend, rrecv, rbias, zbuf, zbias, gbuf, gbias,
    load_sem, tile_sem, p_sem, a_sem, h_sem, b_sem, r_sem, rb_sem, z_sem, zb_sem, g_sem, gb_sem,
    relay_sem,
):
    n_z = n_dom // GROUP
    hall = (hall0, hall1, hall2, hall3)
    dom = lax.axis_index("dom")
    feat = lax.axis_index("feat")
    z = dom // GROUP
    lane = lax.rem(dom, GROUP)
    core = lax.rem(dom, 2)
    partner = (dom + 1 - 2 * core, feat)

    def dom_at(step):
        return lax.rem(dom + (step % n_dom), n_dom)

    def feat_at(hop):
        return lax.rem(feat // 2 + hop[0], NFEAT // 2) * 2 + lax.rem(feat + hop[1], 2)

    def z_at(step):
        return lax.rem(z + step, n_z)

    def z_peer(step):
        return (z_at(step) * GROUP + lane, feat)

    def group_peer(step):
        return (z * GROUP + lax.rem(lane + step, GROUP), feat)

    def around(*distances):
        return sorted({d % n_z for r in distances for d in (r, -r)} - {0})

    barrier = pltpu.get_barrier_semaphore()

    def signal(sem, device):
        pl.semaphore_signal(sem, inc=1, device_id=device, device_id_type=MESH)

    near = [(dom_at(step), feat) for step in range(1, REACH)]
    near += [(dom_at(-step), feat) for step in range(1, REACH)]
    near += [(dom, feat_at(hop)) for hop in HOPS]
    near += [z_peer(step) for step in around(1, 2)]
    for device in near:
        signal(barrier, device)

    pairs = [
        (src_hbm, src), (dst_hbm, dst), (nf_hbm, nf),
        (wt_hbm, wt), (bias_hbm, bias), (og_hbm, og),
    ]
    loads = [pltpu.make_async_copy(a, b, load_sem.at[i]) for i, (a, b) in enumerate(pairs)]
    tile_loads = [
        pltpu.make_async_copy(tiles_hbm.at[:, o], tiles.at[o], tile_sem.at[o])
        for o in range(REACH)
    ]
    for load in loads[:3]:
        load.start()
    for o in ORDER:
        tile_loads[o].start()
    for load in loads[3:]:
        load.start()

    def send(src_ref, dst_ref, sems, device, r=1):
        pltpu.make_async_remote_copy(
            src_ref=src_ref,
            dst_ref=dst_ref,
            send_sem=sems.at[0],
            recv_sem=sems.at[r],
            device_id=device,
            device_id_type=MESH,
        ).start()

    def sent(ref, sems):
        pltpu.make_async_copy(ref, ref, sems.at[0]).wait()

    def arrival(ref, sems, r=1):
        pltpu.make_async_copy(ref, ref, sems.at[r]).wait()

    one = jnp.ones((FW, BLOCK), BF16)
    zero = jnp.zeros((FW, BLOCK), BF16)
    for g in range(NB + 1):
        for row in range(NB):
            table[g, row * FW : (row + 1) * FW, :] = one if row == g else zero

    rows = lax.broadcasted_iota(jnp.int32, (FW, BLOCK), 0)
    columns = lax.broadcasted_iota(jnp.int32, (FW, BLOCK), 1)
    pick = jnp.where(columns == rows + feat * FW, 1.0, 0.0).astype(BF16)
    for load in loads[:3]:
        load.wait()
    picked = lax.dot_general(
        pick, nf[...], (((1,), (1,)), ((), ())), preferred_element_type=F32
    ).astype(BF16)
    for b in range(NB):
        nft[b] = picked[:, b * BLOCK : (b + 1) * BLOCK]

    used = cnt[0]

    def placed(block, position, k):
        position = jnp.where(k < used, position, NB)
        return jnp.concatenate([block] * NB, axis=0) * table[position]

    def forward(o):
        left = []
        right = []
        for j in range(PER_OFFSET):
            k = j * REACH + o
            left.append(placed(nft[src[k]], dst[k] & (NB - 1), k))
            right.append(tiles[o, j])
        return lax.dot_general(
            jnp.concatenate(left, axis=1),
            jnp.concatenate(right, axis=1),
            (((1,), (1,)), ((), ())),
            preferred_element_type=F32,
        )

    for o in ORDER[:-1]:
        tile_loads[o].wait()
        part = forward(o).astype(BF16)
        for part_no in PIECES:
            psend[part_no, o - 1] = part[part_no * ROWS : (part_no + 1) * ROWS, :]
    pl.semaphore_wait(barrier, len(near))
    for part_no in PIECES:
        for o in ORDER[:-1]:
            send(
                psend.at[part_no, o - 1], precv.at[part_no, o - 1], p_sem, (dom_at(o), feat), 1 + part_no
            )
    for step in around(2):
        signal(relay_sem.at[0], z_peer(step))
    tile_loads[0].wait()
    own = forward(0)
    for load in loads[3:]:
        load.wait()
    bias_square = jnp.broadcast_to(bias[...], (HID_DEV, HID_DEV))
    on_diagonal = lax.broadcasted_iota(jnp.int32, (HID_DEV, HID_DEV), 0) == (
        lax.broadcasted_iota(jnp.int32, (HID_DEV, HID_DEV), 1)
    )
    bias_column = jnp.sum(jnp.where(on_diagonal, bias_square, 0.0), axis=1, keepdims=True)
    for part_no in PIECES:
        arrival(precv.at[part_no], p_sem, 1 + part_no)
        piece = own[part_no * ROWS : (part_no + 1) * ROWS, :]
        for o in ORDER[:-1]:
            piece = piece + precv[part_no, o - 1].astype(F32)
        agg[part_no, feat] = piece.astype(BF16)
        for hop in HOPS:
            send(
                agg.at[part_no, feat], agg.at[part_no, feat], a_sem, (dom, feat_at(hop)), 1 + part_no
            )
    if around(2):
        pl.semaphore_wait(relay_sem.at[0], len(around(2)))
    for step in around(4):
        signal(relay_sem.at[1], z_peer(step))

    def send_back(grad_pre, part_no):
        back = lax.dot_general(
            wt[...], grad_pre, (((0,), (0,)), ((), ())), preferred_element_type=F32
        ).astype(BF16)
        for i in range(NFEAT):
            for g in range(SPAN):
                hsend[part_no, i, g * FW : (g + 1) * FW, :] = back[
                    i * FW : (i + 1) * FW, g * BLOCK : (g + 1) * BLOCK
                ]
        for hop in HOPS:
            send(
                hsend.at[part_no, feat_at(hop)], hrecv.at[part_no, feat], h_sem,
                (dom, feat_at(hop)), 1 + part_no,
            )
        hrecv[part_no, feat] = hsend[part_no, feat]

    weight_part = jnp.zeros((HID_DEV, BLOCK), F32)
    bias_part = jnp.zeros((8, BLOCK), F32)
    for part_no in PIECES:
        arrival(agg.at[part_no, 0 : NFEAT - 1], a_sem, 1 + part_no)
        aggregated = jnp.concatenate(
            [
                jnp.concatenate(
                    [agg[part_no, i, g * FW : (g + 1) * FW, :] for i in range(NFEAT)], axis=0
                )
                for g in range(SPAN)
            ],
            axis=1,
        )
        nodes = slice(part_no * SPAN * BLOCK, (part_no + 1) * SPAN * BLOCK)
        pre = jnp.dot(wt[...], aggregated, preferred_element_type=F32) + bias_column
        sigmoid_pre = jax.nn.sigmoid(pre)
        grad_pre = (
            og[:, nodes].astype(F32) * sigmoid_pre * (1.0 + pre * (1.0 - sigmoid_pre))
        ).astype(BF16)
        if part_no < PIECES[-1]:
            send_back(grad_pre, part_no)
        out[:, nodes] = (pre * sigmoid_pre).astype(BF16)
        weight_part = weight_part + lax.dot_general(
            grad_pre, aggregated, (((1,), (1,)), ((), ())), preferred_element_type=F32
        )
        bias_part = bias_part + lax.dot_general(
            jnp.ones((8, SPAN * BLOCK), BF16),
            jnp.concatenate([grad_pre] * 4, axis=0),
            (((1,), (1,)), ((), ())),
            preferred_element_type=F32,
        )
    rsend[0] = weight_part[0:16, :]
    rsend[1] = weight_part[16:32, :]
    rbias[0] = bias_part[0:1, :]
    send(rsend.at[1 - core], rrecv, r_sem, partner)
    send(rbias.at[0], rbias.at[1], rb_sem, partner)

    send_back(grad_pre, PIECES[-1])

    if around(4):
        pl.semaphore_wait(relay_sem.at[1], len(around(4)))
    arrival(rrecv, r_sem)
    arrival(rbias.at[1], rb_sem)
    zbuf[z] = (rsend[core] + rrecv[...]).astype(BF16)
    zbias[z] = rbias[0] + rbias[1]
    far_first = sorted(range(1, n_z), key=lambda step: -min(step, n_z - step))
    for step in far_first:
        send(zbuf.at[z], zbuf.at[z], z_sem, z_peer(step))
        send(zbias.at[z], zbias.at[z], zb_sem, z_peer(step))

    for part_no in PIECES:
        arrival(hrecv.at[part_no, 0 : NFEAT - 1], h_sem, 1 + part_no)
        mixed = hrecv[part_no, 0].astype(F32)
        for i in range(1, NFEAT):
            mixed = mixed + hrecv[part_no, i].astype(F32)
        mixed = mixed.astype(BF16)
        first = part_no * SPAN
        for g in range(SPAN):
            hall0[first + g] = mixed[g * FW : (g + 1) * FW, :]
        blocks = pl.ds(first, SPAN)
        for o in ORDER[:-1]:
            send(hall0.at[blocks], hall[o].at[blocks], b_sem, (dom_at(-o), feat), o)

    def backward(o):
        left = []
        for j in range(PER_OFFSET):
            k = j * REACH + o
            left.append(placed(hall[o][dst[k] & (NB - 1)], src[k], k))
        return jnp.dot(
            jnp.concatenate(left, axis=1),
            tiles[o].reshape(PER_OFFSET * BLOCK, BLOCK),
            preferred_element_type=F32,
        )

    total = backward(0)
    arrival(zbuf.at[0 : n_z - 1], z_sem)
    gbuf[lane] = jnp.sum(zbuf[...].astype(F32), axis=0)
    for step in range(1, GROUP):
        send(gbuf.at[lane], gbuf.at[lane], g_sem, group_peer(step))
    arrival(zbias.at[0 : n_z - 1], zb_sem)
    gbias[lane] = jnp.sum(zbias[...], axis=0)
    for step in range(1, GROUP):
        send(gbias.at[lane], gbias.at[lane], gb_sem, group_peer(step))
    for o in (1, 2, 3):
        arrival(hall[o], b_sem, o)
        total = total + backward(o)
    total = total.astype(BF16)
    for g in range(NB):
        ig[:, g * BLOCK : (g + 1) * BLOCK] = total[g * FW : (g + 1) * FW, :]

    arrival(gbuf.at[0 : GROUP - 1], g_sem)
    arrival(gbias.at[0 : GROUP - 1], gb_sem)
    wg[0:16, :] = gbuf[0] + gbuf[2]
    wg[16:32, :] = gbuf[1] + gbuf[3]
    bg[...] = (gbias[0] + gbias[2])[:, 0:HID_DEV]
    sent(psend, p_sem)
    sent(agg.at[:, 0 : NFEAT - 1], a_sem)
    sent(rsend.at[0], r_sem)
    sent(rbias.at[0], rb_sem)
    sent(hsend.at[:, 0 : NFEAT - 1], h_sem)
    sent(zbuf.at[0 : n_z - 1], z_sem)
    sent(zbias.at[0 : n_z - 1], zb_sem)
    sent(psend, b_sem)
    sent(gbuf.at[0 : GROUP - 1], g_sem)
    sent(gbias.at[0 : GROUP - 1], gb_sem)


def finish(*refs):
    values, outs, sem = refs[:4], refs[4:8], refs[8]
    copies = [pltpu.make_async_copy(a, b, sem.at[i]) for i, (a, b) in enumerate(zip(values, outs))]
    for copy in copies:
        copy.start()
    for copy in copies:
        copy.wait()


def shards(node_features, weight, bias, tile_values, tile_src, tile_dst, tile_counts, out_grad):
    n_dom = lax.axis_size("dom")
    n_z = n_dom // GROUP
    nodes = NB * BLOCK
    vmem = pl.BlockSpec(memory_space=pltpu.VMEM)
    hbm = pl.BlockSpec(memory_space=pltpu.HBM)
    anywhere = pl.BlockSpec(memory_space=pl.ANY)
    dma = pltpu.SemaphoreType.DMA
    block = pltpu.VMEM((NB, FW, BLOCK), BF16)
    square = pltpu.VMEM((len(PIECES), NFEAT, ROWS, BLOCK), BF16)
    limit = 24 * 1024 * 1024
    shapes = (
        jax.ShapeDtypeStruct((HID_DEV, nodes), BF16),
        jax.ShapeDtypeStruct((HID_DEV, BLOCK), F32),
        jax.ShapeDtypeStruct((1, HID_DEV), F32),
        jax.ShapeDtypeStruct((FW, nodes), BF16),
    )
    results = pl.pallas_call(
        functools.partial(kernel, n_dom),
        out_shape=shapes,
        in_specs=[hbm] * 6 + [pl.BlockSpec(memory_space=pltpu.SMEM), hbm],
        out_specs=(vmem,) * 4,
        scratch_shapes=[
            pltpu.VMEM((nodes, BLOCK), BF16),
            pltpu.VMEM((HID_DEV, nodes), BF16),
            pltpu.VMEM((HID_DEV, BLOCK), BF16),
            pltpu.VMEM((1, HID_DEV), F32),
            pltpu.SMEM((PER_OFFSET * REACH,), jnp.int32),
            pltpu.SMEM((PER_OFFSET * REACH,), jnp.int32),
            pltpu.VMEM((REACH, PER_OFFSET, BLOCK, BLOCK), BF16),
            block,
            pltpu.VMEM((NB + 1, BLOCK, BLOCK), BF16),
            pltpu.VMEM((len(PIECES), REACH - 1, ROWS, BLOCK), BF16),
            pltpu.VMEM((len(PIECES), REACH - 1, ROWS, BLOCK), BF16),
            square,
            square,
            square,
            block,
            block,
            block,
            block,
            pltpu.VMEM((2, 16, BLOCK), F32),
            pltpu.VMEM((16, BLOCK), F32),
            pltpu.VMEM((2, 1, BLOCK), F32),
            pltpu.VMEM((n_z, 16, BLOCK), BF16),
            pltpu.VMEM((n_z, 1, BLOCK), F32),
            pltpu.VMEM((GROUP, 16, BLOCK), F32),
            pltpu.VMEM((GROUP, 1, BLOCK), F32),
            dma((6,)),
            dma((REACH,)),
            dma((5,)),
            dma((5,)),
            dma((5,)),
            dma((REACH,)),
            dma((2,)),
            dma((2,)),
            dma((2,)),
            dma((2,)),
            dma((2,)),
            dma((2,)),
            pltpu.SemaphoreType.REGULAR((2,)),
        ],
        compiler_params=pltpu.CompilerParams(
            collective_id=0, has_side_effects=True, vmem_limit_bytes=limit
        ),
        name="graph_layer",
    )(
        *(
            x if x is tile_counts else pltpu.with_memory_space_constraint(x, pltpu.HBM)
            for x in (
                node_features,
                weight.T,
                bias.reshape(1, HID_DEV),
                tile_values.reshape(PER_OFFSET, REACH, BLOCK, BLOCK),
                tile_src,
                tile_dst,
                tile_counts,
                out_grad.T,
            )
        )
    )
    out, wg, bg, ig = pl.pallas_call(
        finish,
        out_shape=shapes,
        in_specs=[anywhere] * 4,
        out_specs=(hbm,) * 4,
        scratch_shapes=[dma((4,))],
        compiler_params=pltpu.CompilerParams(vmem_limit_bytes=1024 * 1024),
        name="store_outputs",
    )(*results)
    return out.T, wg.T, bg.reshape(HID_DEV), ig.T


def solution(mesh):
    return jax.shard_map(
        shards,
        mesh=mesh,
        in_specs=(
            P("dom", None),
            P(None, "feat"),
            P("feat"),
            P("dom", None, None),
            P("dom"),
            P("dom"),
            P("dom"),
            P("dom", "feat"),
        ),
        out_specs=(P("dom", "feat"), P(None, "feat"), P("feat"), P("dom", "feat")),
        check_vma=False,
    )
```
